32 devices in a mesh: seq: 4 (over z), expert: 8 (over y, x, core).
Axes of the slice: x: 2, y: 2, z: 4, core: 2. Of those that a mesh axis runs over, the one named last changes fastest.
Arguments:
- tokens: bfloat16 [2, 4096, 1280], P(None, 'seq'), may hold values from -46.205783 to 46.205783
- slot_embed: bfloat16 [1280, 256], P(None, 'expert'), may hold values from -0.14115179 to 0.14115179
- combine: bfloat16 [2, 4096, 256], P(None, 'seq', 'expert'), may hold values from 0.0009765625 to 0.015625
- w_in: bfloat16 [8, 1280, 5120], P('expert', None, 'seq'), may hold values from -0.15625 to 0.15625
- w_out: bfloat16 [8, 5120, 1280], P('expert', 'seq'), may hold values from -0.078125 to 0.078125
- grad_out: bfloat16 [2, 4096, 1280], P(None, 'seq'), may hold values from -6 to 6
Outputs:
- grad_tokens: bfloat16 [2, 4096, 1280], P(None, ('seq', 'expert'))
- grad_embed: bfloat16 [1280, 256], P('seq', 'expert')
- grad_w_in: bfloat16 [8, 1280, 5120], P('expert', None, 'seq')
- grad_w_out: bfloat16 [8, 5120, 1280], P('expert', 'seq')
The draws below stay inside these ranges and needn't reach their ends.
All inputs are finite; a program needn't handle non-finite values.
Results may differ from the reference program's by a relative error of at most 0.028.
Values may be sent and summed in bfloat16 or wider, within the bound.
A program may use at most 128 MiB of HBM per device.

```python
import math
import jax
import jax.numpy as jnp
from jax import lax

D = 1280
HID = 5120
SLOTS = 32
IMAGES = 2
LEN = 4096
EXPERTS = 8


def shared_embed(key):
    normal_part = jax.random.normal(jax.random.fold_in(key, 11), (D, EXPERTS * SLOTS), jnp.float32)
    return jnp.clip(normal_part, -5.0, 5.0) * D ** (-0.5)


def draw_slot_embed(key, part):
    return shared_embed(key).astype(jnp.bfloat16)


def position_ramp(start, ratio):
    position = jnp.arange(LEN, dtype=jnp.float32) / float(max(LEN - 1, 1))
    return (start * jnp.exp(math.log(ratio) * position))[None, :, None]


def draw_tokens(key, part):
    noise_key = jax.random.fold_in(key, 12)
    background = jax.random.normal(noise_key, (IMAGES, LEN, D), jnp.float32)
    background = jnp.clip(background, -6.0, 6.0) * position_ramp(0.8, 2.25)
    return background.astype(jnp.bfloat16)


def block_scale(stream_key, shape, cuts, low, largest):
    gain, own = 1.0, jax.random.fold_in(stream_key, 6)
    for dim, blocks in cuts:
        steps = jnp.exp(jax.random.uniform(jax.random.fold_in(own, dim), (blocks,), jnp.float32, low / len(cuts), largest / len(cuts)))
        gain = gain * jnp.repeat(steps, shape[dim] // blocks).reshape([-1 if axis == dim else 1 for axis in range(len(shape))])
    return gain


def noise(rng, extent, spread, most, split=(), kind=jnp.bfloat16):
    result = spread * jax.random.normal(rng, extent, jnp.float32)
    if split:
        result = result * block_scale(rng, extent, split, -0.22, 0.18)
    return jnp.clip(result, -most, most).astype(kind)


def setup_inputs(seed: int = 0) -> dict:
    key_of = jax.random.split(jax.random.key(seed), 7)
    tokens = draw_tokens(jax.random.fold_in(key_of[6], 71), 0)
    slot_embed = draw_slot_embed(jax.random.fold_in(key_of[6], 71), 0)
    combine = jnp.clip(jnp.exp(math.log(0.015625) - 2.7725887 * jax.random.uniform(key_of[2], (IMAGES, LEN, EXPERTS * SLOTS), jnp.float32) ** block_scale(key_of[2], (IMAGES, LEN, EXPERTS * SLOTS), ((1, 4), (2, 8)), -0.2, 0.2)), 0.0009765625, 0.015625).astype(jnp.bfloat16)
    w_in = noise(key_of[3], (EXPERTS, D, HID), D ** -0.5, 0.15625, ((0, 8), (2, 4)))
    w_out = noise(key_of[4], (EXPERTS, HID, D), HID ** -0.5, 0.078125, ((0, 8), (1, 4)))
    grad_out = noise(key_of[5], (IMAGES, LEN, D), 1.0, 6.0, ((1, 4),))
    return {"tokens": tokens, "slot_embed": slot_embed, "combine": combine, "w_in": w_in, "w_out": w_out, "grad_out": grad_out}


def gelu_exact(values):
    return 0.5 * values * (1.0 + jax.scipy.special.erf(values / math.sqrt(2.0)))

def gelu_slope(values):
    return 0.5 * (1.0 + jax.scipy.special.erf(values / math.sqrt(2.0))) + values * jnp.exp(-0.5 * values * values) / math.sqrt(2.0 * math.pi)

def reference(tokens, slot_embed, combine, w_in, w_out, grad_out):
    tokens_full = tokens.astype(jnp.float32)
    embed_full = slot_embed.astype(jnp.float32)
    combine_full = combine.astype(jnp.float32)
    grad_full = grad_out.astype(jnp.float32)
    w_in_full = w_in.astype(jnp.float32)
    w_out_full = w_out.astype(jnp.float32)
    logits = jnp.einsum('itd,dj->itj', tokens_full, embed_full)
    col_peak = lax.optimization_barrier(jnp.max(logits, axis=1, keepdims=True))
    exponent = jnp.exp(logits - col_peak)
    dispatch = (exponent / lax.optimization_barrier(jnp.sum(exponent, axis=1, keepdims=True))).astype(jnp.bfloat16)
    dispatch_full = dispatch.astype(jnp.float32)
    slot_in = jnp.einsum('itj,itd->ijd', dispatch_full, tokens_full).astype(jnp.bfloat16)
    slot_in = slot_in.reshape(IMAGES, EXPERTS, SLOTS, D).astype(jnp.float32)
    pre_act = jnp.einsum('iesd,edh->iesh', slot_in, w_in_full)
    act_value = gelu_exact(pre_act).astype(jnp.bfloat16).astype(jnp.float32)
    slot_out = jnp.einsum('iesh,ehd->iesd', act_value, w_out_full).astype(jnp.bfloat16)
    slot_out = slot_out.reshape(IMAGES, EXPERTS * SLOTS, D).astype(jnp.float32)
    grad_combine = jnp.einsum('itd,ijd->itj', grad_full, slot_out)
    row_dot = lax.optimization_barrier(jnp.sum(combine_full * grad_combine, axis=2, keepdims=True))
    grad_slot_out = jnp.einsum('itj,itd->ijd', combine_full, grad_full).astype(jnp.bfloat16)
    grad_slot_out = grad_slot_out.reshape(IMAGES, EXPERTS, SLOTS, D).astype(jnp.float32)
    grad_act = jnp.einsum('iesd,ehd->iesh', grad_slot_out, w_out_full)
    grad_pre = (grad_act * gelu_slope(pre_act)).astype(jnp.bfloat16).astype(jnp.float32)
    grad_w_out = jnp.einsum('iesh,iesd->ehd', act_value, grad_slot_out).astype(jnp.bfloat16)
    grad_w_in = jnp.einsum('iesd,iesh->edh', slot_in, grad_pre).astype(jnp.bfloat16)
    grad_slot_in = jnp.einsum('iesh,edh->iesd', grad_pre, w_in_full).astype(jnp.bfloat16)
    grad_slot_in = grad_slot_in.reshape(IMAGES, EXPERTS * SLOTS, D).astype(jnp.float32)
    grad_dispatch = jnp.einsum('itd,ijd->itj', tokens_full, grad_slot_in)
    col_dot = lax.optimization_barrier(jnp.sum(dispatch_full * grad_dispatch, axis=1, keepdims=True))
    grad_logits = (dispatch_full * (grad_dispatch - col_dot) + combine_full * (grad_combine - row_dot)).astype(jnp.bfloat16)
    logits_full = grad_logits.astype(jnp.float32)
    grad_embed = jnp.einsum('itd,itj->dj', tokens_full, logits_full).astype(jnp.bfloat16)
    grad_tokens = jnp.einsum('itj,ijd->itd', dispatch_full, grad_slot_in) + jnp.einsum('itj,dj->itd', logits_full, embed_full)
    return (grad_tokens.astype(jnp.bfloat16), grad_embed, grad_w_in, grad_w_out)
```

```python
import functools
import math

import jax
import jax.numpy as jnp
from jax import lax
from jax.experimental import pallas as pl
from jax.experimental.pallas import tpu as pltpu
from jax.sharding import PartitionSpec as P

MESH = pl.DeviceIdType.MESH
BF16 = jnp.bfloat16
F32 = jnp.float32

Z_STAT, Z_IN, Z_INF, Z_GRAD, Z_GRADF, Z_OUT, Z_OUTF, Z_GIN, Z_GINF, Z_COL, Z_EMB, Z_KINDS = range(12)
E_EMB, E_DISP, E_ROW, E_GIN, E_LOG, E_KINDS = range(6)
L_EMB, L_COMB, L_WIN, L_WOUT, L_TOK, L_GO, L_KINDS = 0, 1, 2, 3, 4, 6, 8


def nn(a, b):
    return lax.dot_general(a, b, (((1,), (0,)), ((), ())), preferred_element_type=F32)


def nt(a, b):
    return lax.dot_general(a, b, (((1,), (1,)), ((), ())), preferred_element_type=F32)


def tn(a, b):
    return lax.dot_general(a, b, (((0,), (0,)), ((), ())), preferred_element_type=F32)


def gelu_parts(v):
    half = 0.5 * (1.0 + lax.erf(v * (1.0 / math.sqrt(2.0))))
    return half, v * jnp.exp(-0.5 * v * v) * (1.0 / math.sqrt(2.0 * math.pi))


def flip(index, k):
    out = index
    bit = 1
    while bit <= k:
        if k & bit:
            out = out + bit * (1 - 2 * ((index // bit) % 2))
        bit *= 2
    return out


def main_kernel(
    S, E,
    emb_h, tok_h, comb_h, go_h, win_h, wout_h,
    gt_ref, ge_ref, act_ref, gso_ref, sin_ref, gpre_ref,
    emb, tok, go, win, wout,
    emb_all, disp_all, gin_all, log_all, dsend, lsend, row_buf,
    prob, disp, combt, gcomb, gdisp, weight, statbuf, colbuf,
    part_in, part_grad, part_out, part_gin,
    rs_in, rs_grad, rs_out, rs_gin,
    full_in, full_grad, full_out, full_gin,
    pre, esend, erecv, embed_send, embed_recv,
    zs, zr, es, er, ls,
):
    images, patches, width = tok.shape
    slots = combt.shape[1]
    rows = images * slots
    own = rows // S
    tl = patches // E
    s = lax.axis_index("seq")
    e = lax.axis_index("expert")
    zpeer = [flip(s, k) for k in range(S)]
    epeer = [flip(e, k) for k in range(E)]

    loads = {}

    def load(key, src, dst):
        loads[key] = pltpu.make_async_copy(src, dst, ls.at[key])
        loads[key].start()

    load(L_EMB, emb_h, emb)
    for i in range(images):
        load(L_TOK + i, tok_h.at[i], tok.at[i])
    load(L_COMB, comb_h, combt)
    for i in range(images):
        load(L_GO + i, go_h.at[i], go.at[i])
    load(L_WIN, win_h, win)
    load(L_WOUT, wout_h, wout)

    barrier = pltpu.get_barrier_semaphore()
    for k in range(1, S):
        pl.semaphore_signal(barrier, inc=1, device_id=(zpeer[k], e), device_id_type=MESH)
    for k in range(1, E):
        pl.semaphore_signal(barrier, inc=1, device_id=(s, epeer[k]), device_id_type=MESH)

    sent = []

    def zcopy(kind, k, src, dst):
        return pltpu.make_async_remote_copy(
            src_ref=src, dst_ref=dst, send_sem=zs.at[kind, k], recv_sem=zr.at[kind, k],
            device_id=(zpeer[k], e), device_id_type=MESH)

    def ecopy(kind, k, src, dst, to=None):
        return pltpu.make_async_remote_copy(
            src_ref=src, dst_ref=dst, send_sem=es.at[kind, k], recv_sem=er.at[kind, k],
            device_id=(s, epeer[k if to is None else to]), device_id_type=MESH)

    def start(group):
        for c in group:
            c.start()
        sent.extend(group)
        return group

    def arrive(group):
        for c in group:
            c.wait_recv()

    def scatter(kind, part, into):
        return start([
            zcopy(kind, k, part.at[pl.ds(pl.multiple_of(zpeer[k] * own, own), own)], into.at[k - 1])
            for k in range(1, S)])

    mine = pl.ds(pl.multiple_of(s * own, own), own)

    def gather(kind, full):
        return start([zcopy(kind, k, full.at[mine], full.at[mine]) for k in range(1, S)])

    def owned_sum(part, into):
        total = part[mine].astype(F32)
        for k in range(1, S):
            total = total + into[k - 1].astype(F32)
        return total.astype(BF16)

    loads[L_EMB].wait()
    emb_rows = emb[...]
    emb_all[0] = emb_rows

    peaks, totals = [], []
    for i in range(images):
        loads[L_TOK + i].wait()
        logits = nt(emb_rows, tok[i])
        peak = jnp.max(logits, axis=1, keepdims=True)
        value = jnp.exp(logits - peak)
        prob[i] = value
        peaks.append(peak)
        totals.append(jnp.sum(value, axis=1, keepdims=True))
        part_in[i * slots:(i + 1) * slots] = nn(value.astype(BF16), tok[i]).astype(BF16)
    colbuf[...] = jnp.zeros_like(colbuf)
    statbuf[8 * S:] = jnp.zeros_like(statbuf[8 * S:])
    for i in range(images):
        colbuf[i * slots:(i + 1) * slots] = jnp.broadcast_to(peaks[i], (slots, 128))
        colbuf[rows + i * slots:rows + (i + 1) * slots] = jnp.broadcast_to(totals[i], (slots, 128))
    statbuf[0:8] = colbuf[...].T[0:8]

    pl.semaphore_wait(barrier, S - 1 + E - 1)
    stats = start([zcopy(Z_STAT, k, statbuf.at[pl.ds(0, 8)], statbuf.at[pl.ds(8 * k, 8)])
                   for k in range(1, S)])
    in_rs = scatter(Z_IN, part_in, rs_in)
    emb_ag = start([ecopy(E_EMB, k, emb_all.at[0], emb_all.at[k]) for k in range(1, E)])

    loads[L_COMB].wait()
    for i in range(images):
        loads[L_GO + i].wait()
        part_grad[i * slots:(i + 1) * slots] = nn(combt[i], go[i]).astype(BF16)
    grad_rs = scatter(Z_GRAD, part_grad, rs_grad)

    arrive(stats)
    cols = statbuf[...].T
    peak_of = [cols[0:rows, 8 * k:8 * k + 1] for k in range(S)]
    total_of = [cols[rows:2 * rows, 8 * k:8 * k + 1] for k in range(S)]
    top = peak_of[0]
    for k in range(1, S):
        top = jnp.maximum(top, peak_of[k])
    scale = [jnp.exp(p - top) for p in peak_of]
    denom = scale[0] * total_of[0]
    for k in range(1, S):
        denom = denom + scale[k] * total_of[k]
    for k in range(S):
        weight[k] = jnp.broadcast_to(scale[k] / denom, (rows, 128))
    arrive(in_rs)
    total = part_in[mine].astype(F32) * weight[0, mine][:, 0:1]
    for k in range(1, S):
        total = total + rs_in[k - 1].astype(F32) * weight[k, mine][:, 0:1]
    full_in[mine] = total.astype(BF16)
    in_ag = gather(Z_INF, full_in)

    for i in range(images):
        d = (prob[i] * weight[0, i * slots:(i + 1) * slots][:, 0:1]).astype(BF16)
        disp[i] = d
        for g in range(E):
            dsend[g, i * slots:(i + 1) * slots] = d[:, g * tl:(g + 1) * tl]
    disp_all[0] = dsend[e]
    disp_a2a = start([ecopy(E_DISP, k, dsend.at[epeer[k]], disp_all.at[k]) for k in range(1, E)])

    arrive(grad_rs)
    full_grad[mine] = owned_sum(part_grad, rs_grad)
    grad_ag = gather(Z_GRADF, full_grad)

    arrive(in_ag)
    loads[L_WIN].wait()
    v = nn(full_in[...], win[0])
    half, slope = gelu_parts(v)
    act = (v * half).astype(BF16)
    act_ref[...] = act
    pre[...] = half + slope
    loads[L_WOUT].wait()
    part_out[...] = nn(act, wout[0]).astype(BF16)
    out_rs = scatter(Z_OUT, part_out, rs_out)
    arrive(grad_ag)
    grad_pre = (nt(full_grad[...], wout[0]) * pre[...]).astype(BF16)
    gpre_ref[...] = grad_pre
    part_gin[...] = nt(grad_pre, win[0]).astype(BF16)
    gin_rs = scatter(Z_GIN, part_gin, rs_gin)
    arrive(out_rs)
    full_out[mine] = owned_sum(part_out, rs_out)
    out_ag = gather(Z_OUTF, full_out)
    sin_ref[...] = full_in[...]
    gso_ref[...] = full_grad[...]
    arrive(gin_rs)
    full_gin[mine] = owned_sum(part_gin, rs_gin)
    gin_ag = gather(Z_GINF, full_gin)

    arrive(out_ag)
    per_row = 8 // images
    row_width = patches // per_row
    for i in range(images):
        gc = nt(full_out[i * slots:(i + 1) * slots], go[i])
        gcomb[i] = gc
        rd = jnp.sum(combt[i].astype(F32) * gc, axis=0, keepdims=True)
        for q in range(per_row):
            row_buf[0, i * per_row + q:i * per_row + q + 1] = rd[:, q * row_width:(q + 1) * row_width]
    row_x = start([ecopy(E_ROW, k, row_buf.at[0], row_buf.at[k]) for k in range(1, E)])

    arrive(gin_ag)
    gin_all[0] = full_gin[...]
    gin_x = start([ecopy(E_GIN, k, gin_all.at[0], gin_all.at[k])
                   for k in [1] + list(range(2, E, 2))])
    for i in range(images):
        gd = nt(full_gin[i * slots:(i + 1) * slots], tok[i])
        gdisp[i] = gd
        cd = jnp.sum(disp[i].astype(F32) * gd, axis=1, keepdims=True)
        colbuf[i * slots:(i + 1) * slots] = jnp.broadcast_to(cd, (slots, 128))
    esend[...] = colbuf[...].T[0:8]
    col_x = start([zcopy(Z_COL, k, esend, erecv.at[k - 1]) for k in range(1, S)])
    arrive(row_x)
    row_total = row_buf[0]
    for k in range(1, E):
        row_total = row_total + row_buf[k]
    for i in range(images):
        rd = jnp.concatenate(
            [row_total[i * per_row + q:i * per_row + q + 1] for q in range(per_row)], axis=1)
        gcomb[i] = combt[i].astype(F32) * (gcomb[i] - rd)
    arrive(col_x)
    col_total = esend[...]
    for k in range(1, S):
        col_total = col_total + erecv[k - 1]
    colbuf[0:8] = col_total
    col_dot = colbuf[...].T[:, 0:1]
    embed_part = None
    grads = []
    for i in range(images):
        gl = (disp[i].astype(F32) * (gdisp[i] - col_dot[i * slots:(i + 1) * slots])
              + gcomb[i]).astype(BF16)
        grads.append(gl)
        for g in range(E):
            lsend[g, i * slots:(i + 1) * slots] = gl[:, g * tl:(g + 1) * tl]
    log_all[0] = lsend[e]
    log_a2a = start([ecopy(E_LOG, k, lsend.at[epeer[k]], log_all.at[k]) for k in range(1, E)])
    for i in range(images):
        term = nn(grads[i], tok[i])
        embed_part = term if embed_part is None else embed_part + term
    return_rows = width // S
    embed_part = embed_part.astype(BF16)
    for g in range(S):
        embed_send[g] = embed_part[:, g * return_rows:(g + 1) * return_rows]
    embed_rs = start([zcopy(Z_EMB, k, embed_send.at[zpeer[k]], embed_recv.at[k - 1])
                      for k in range(1, S)])

    own_gin = {c: x for c, x in zip([1] + list(range(2, E, 2)), gin_x)}
    forward = []
    for k in range(2, E, 2):
        own_gin[k].wait_recv()
        forward += start([ecopy(E_GIN, k + 1, gin_all.at[k], gin_all.at[k + 1], to=1)])
    own_gin[1].wait_recv()
    arrive(disp_a2a)
    arrive(emb_ag)
    arrive(embed_rs)
    total = embed_send[s].astype(F32)
    for k in range(1, S):
        total = total + embed_recv[k - 1].astype(F32)
    ge_ref[...] = total.astype(BF16)
    arrive(log_a2a)
    arrive(forward)
    every = emb_all[...].reshape(E * slots, width)
    for i in range(images):
        here = slice(i * slots, (i + 1) * slots)
        gt = tn(log_all[:, here].reshape(E * slots, tl), every)
        gt = gt + tn(disp_all[:, here].reshape(E * slots, tl),
                     gin_all[:, here].reshape(E * slots, width))
        gt_ref[i] = gt.astype(BF16)
    for c in sent:
        c.wait_send()


def weights_kernel(sin, gpre, act, gso, gw_in, gw_out):
    gw_in[0] = tn(sin[...], gpre[...]).astype(BF16)
    gw_out[0] = tn(act[...], gso[...]).astype(BF16)


def local(S, E, tokens, slot_embed, combine, w_in, w_out, grad_out):
    images, patches, width = tokens.shape
    slots = slot_embed.shape[1]
    hidden = w_in.shape[2]
    rows = images * slots
    own = rows // S
    tl = patches // E
    any_spec = pl.BlockSpec(memory_space=pl.ANY)
    vmem_spec = pl.BlockSpec(memory_space=pltpu.VMEM)

    def shape(*dims, dtype=BF16):
        return jax.ShapeDtypeStruct(dims, dtype)

    def vmem(*dims, dtype=BF16):
        return pltpu.VMEM(dims, dtype)

    flops = 2 * images * patches * slots * width * 7 + 8 * rows * width * hidden
    gt, ge, act, gso, slot_in, gpre = pl.pallas_call(
        functools.partial(main_kernel, S, E),
        out_shape=(
            shape(images, tl, width), shape(slots, width // S), shape(rows, hidden),
            shape(rows, width), shape(rows, width), shape(rows, hidden),
        ),
        in_specs=[any_spec] * 6,
        out_specs=(vmem_spec,) * 6,
        scratch_shapes=[
            vmem(slots, width), vmem(*tokens.shape),
            vmem(*grad_out.shape), vmem(*w_in.shape), vmem(*w_out.shape),
            vmem(E, slots, width), vmem(E, rows, tl), vmem(E, rows, width), vmem(E, rows, tl),
            vmem(E, rows, tl), vmem(E, rows, tl),
            vmem(E, 8, images * patches // 8, dtype=F32),
            vmem(images, slots, patches, dtype=F32), vmem(images, slots, patches),
            vmem(images, slots, patches), vmem(images, slots, patches, dtype=F32),
            vmem(images, slots, patches, dtype=F32),
            vmem(S, rows, 128, dtype=F32), vmem(128, 128, dtype=F32), vmem(128, 128, dtype=F32),
            vmem(rows, width), vmem(rows, width), vmem(rows, width), vmem(rows, width),
            vmem(S - 1, own, width), vmem(S - 1, own, width),
            vmem(S - 1, own, width), vmem(S - 1, own, width),
            vmem(rows, width), vmem(rows, width), vmem(rows, width), vmem(rows, width),
            vmem(rows, hidden, dtype=F32),
            vmem(8, 128, dtype=F32), vmem(S - 1, 8, 128, dtype=F32),
            vmem(S, slots, width // S), vmem(S - 1, slots, width // S),
            pltpu.SemaphoreType.DMA((Z_KINDS, S)), pltpu.SemaphoreType.DMA((Z_KINDS, S)),
            pltpu.SemaphoreType.DMA((E_KINDS, E)), pltpu.SemaphoreType.DMA((E_KINDS, E)),
            pltpu.SemaphoreType.DMA((L_KINDS,)),
        ],
        compiler_params=pltpu.CompilerParams(
            collective_id=0, has_side_effects=True, vmem_limit_bytes=56 * 2**20),
        cost_estimate=pl.CostEstimate(
            flops=flops, bytes_accessed=18 * 2**20, transcendentals=images * patches * slots),
        name="moe_backward",
    )(slot_embed.T, tokens, jnp.swapaxes(combine, 1, 2), grad_out, w_in, w_out)

    steps = 5 if width % (5 * 128) == 0 and hidden % (5 * 128) == 0 else 1
    gw_in, gw_out = pl.pallas_call(
        weights_kernel,
        grid=(steps,),
        out_shape=(shape(1, width, hidden), shape(1, hidden, width)),
        in_specs=[
            pl.BlockSpec((rows, width // steps), lambda i: (0, i)),
            pl.BlockSpec((rows, hidden), lambda i: (0, 0)),
            pl.BlockSpec((rows, hidden // steps), lambda i: (0, i)),
            pl.BlockSpec((rows, width), lambda i: (0, 0)),
        ],
        out_specs=(
            pl.BlockSpec((1, width // steps, hidden), lambda i: (0, i, 0)),
            pl.BlockSpec((1, hidden // steps, width), lambda i: (0, i, 0)),
        ),
        compiler_params=pltpu.CompilerParams(vmem_limit_bytes=24 * 2**20),
        name="weight_gradients",
    )(slot_in, gpre, act, gso)
    return gt, ge.T, gw_in, gw_out


def solution(mesh):
    return jax.shard_map(
        functools.partial(local, mesh.shape["seq"], mesh.shape["expert"]),
        mesh=mesh,
        in_specs=(
            P(None, "seq", None),
            P(None, "expert"),
            P(None, "seq", "expert"),
            P("expert", None, "seq"),
            P("expert", "seq", None),
            P(None, "seq", None),
        ),
        out_specs=(
            P(None, ("seq", "expert"), None),
            P("seq", "expert"),
            P("expert", None, "seq"),
            P("expert", "seq", None),
        ),
        check_vma=False,
    )
```

```python
import functools
import math

import jax
import jax.numpy as jnp
from jax import lax
from jax.experimental import pallas as pl
from jax.experimental.pallas import tpu as pltpu
from jax.sharding import PartitionSpec as P

MESH = pl.DeviceIdType.MESH
BF16 = jnp.bfloat16
F32 = jnp.float32

(Z_STAT, Z_IN, Z_INF, Z_GRAD, Z_GRADF, Z_OUT, Z_OUTF, Z_GIN, Z_GINF, Z_COL, Z_EMB,
 Z_KINDS) = range(12)
E_EMB, E_DISP, E_ROW, E_LOG, E_GIN = range(5)


def nn(a, b):
    return lax.dot_general(a, b, (((1,), (0,)), ((), ())), preferred_element_type=F32)


def nt(a, b):
    return lax.dot_general(a, b, (((1,), (1,)), ((), ())), preferred_element_type=F32)


def tn(a, b):
    return lax.dot_general(a, b, (((0,), (0,)), ((), ())), preferred_element_type=F32)


def gelu_parts(v):
    half = 0.5 * (1.0 + lax.erf(v * (1.0 / math.sqrt(2.0))))
    return half, v * jnp.exp(-0.5 * v * v) * (1.0 / math.sqrt(2.0 * math.pi))


def flip(index, k):
    out = index
    bit = 1
    while bit <= k:
        if k & bit:
            out = out + bit * (1 - 2 * ((index // bit) % 2))
        bit *= 2
    return out


def main_kernel(
    S, E,
    emb_h, tok_h, comb_h, go_h, win_h, wout_h,
    gt_h, ge_h, act_h, gso_h, sin_h, gpre_h,
    emb, tok, go, win, wout,
    emb_all, disp_all, gin_all, log_all, dsend, lsend, row_buf,
    prob, disp, combt, gcomb, gdisp, weight, statbuf, colbuf,
    part_in, part_grad, part_out, part_gin,
    rs_in, rs_grad, rs_out, rs_gin,
    full_in, full_grad, full_out, full_gin,
    act, gpre, gt, ge, pre, esend, erecv, embed_send, embed_recv,
    zs, zr, es, er, ls,
):
    images, patches, width = tok.shape
    slots = combt.shape[1]
    tl = patches // E
    rsplit = slots // 16
    csplit = S // rsplit
    cw = width // csplit
    s = lax.axis_index("seq")
    e = lax.axis_index("expert")
    zpeer = [flip(s, k) for k in range(S)]
    epeer = [flip(e, k) for k in range(E)]

    local_copies = []

    def move(src, dst):
        c = pltpu.make_async_copy(src, dst, ls.at[len(local_copies)])
        local_copies.append(c)
        c.start()
        return c

    emb_l = move(emb_h, emb)
    tok_l = [move(tok_h.at[0], tok.at[0])]
    comb_l = move(comb_h, combt)
    go_l = [move(go_h.at[0], go.at[0])]
    for i in range(1, images):
        tok_l.append(move(tok_h.at[i], tok.at[i]))
        go_l.append(move(go_h.at[i], go.at[i]))
    win_l = move(win_h, win)
    wout_l = move(wout_h, wout)
    stores = []

    barrier = pltpu.get_barrier_semaphore()
    for k in range(1, S):
        pl.semaphore_signal(barrier, inc=1, device_id=(zpeer[k], e), device_id_type=MESH)
    for k in range(1, E):
        pl.semaphore_signal(barrier, inc=1, device_id=(s, epeer[k]), device_id_type=MESH)

    sent = []

    def zcopy(kind, i, k, src, dst):
        return pltpu.make_async_remote_copy(
            src_ref=src, dst_ref=dst, send_sem=zs.at[kind * images + i, k],
            recv_sem=zr.at[kind * images + i, k],
            device_id=(zpeer[k], e), device_id_type=MESH)

    def ecopy(kind, k, src, dst, to=None):
        return pltpu.make_async_remote_copy(
            src_ref=src, dst_ref=dst, send_sem=es.at[kind, k], recv_sem=er.at[kind, k],
            device_id=(s, epeer[k if to is None else to]), device_id_type=MESH)

    def start(group):
        for c in group:
            c.start()
        sent.extend(group)
        return group

    def arrive(group):
        for c in group:
            c.wait_recv()

    def part_of(owner):
        return (pl.ds(pl.multiple_of((owner // csplit) * 16, 16), 16),
                pl.ds(pl.multiple_of((owner % csplit) * cw, 128), cw))

    mine = part_of(s)
    theirs = [part_of(p) for p in zpeer]

    def scatter(kind, i, part, into):
        return start([zcopy(kind, i, k, part.at[(i,) + theirs[k]], into.at[i, k - 1])
                      for k in range(1, S)])

    def gather(kind, i, full):
        here = (i,) + mine
        return start([zcopy(kind, i, k, full.at[here], full.at[here]) for k in range(1, S)])

    def sum_and_gather(rs, kind, i, part, into, full):
        arrive(rs)
        here = (i,) + mine
        total = part[here].astype(F32)
        for k in range(1, S):
            total = total + into[i, k - 1].astype(F32)
        full[here] = total.astype(BF16)
        return gather(kind, i, full)

    def softmax(i):
        tok_l[i].wait()
        logits = nt(emb[...], tok[i])
        peak = jnp.max(logits, axis=1, keepdims=True)
        value = jnp.exp(logits - peak)
        prob[i] = value
        part_in[i] = nn(value.astype(BF16), tok[i]).astype(BF16)
        colbuf[0:slots] = jnp.broadcast_to(peak, (slots, 128))
        colbuf[slots:2 * slots] = jnp.broadcast_to(
            jnp.sum(value, axis=1, keepdims=True), (slots, 128))
        statbuf[i, 0:8] = colbuf[...].T[0:8]

    def softmax_send(i):
        st = start([zcopy(Z_STAT, i, k, statbuf.at[i, pl.ds(0, 8)],
                          statbuf.at[i, pl.ds(8 * k, 8)]) for k in range(1, S)])
        return st, scatter(Z_IN, i, part_in, rs_in)

    def out_grads(i):
        go_l[i].wait()
        part_grad[i] = nn(combt[i], go[i]).astype(BF16)
        return scatter(Z_GRAD, i, part_grad, rs_grad)

    def slot_inputs(i, st, rs):
        arrive(st)
        cols = statbuf[i].T
        peak_of = [cols[0:slots, 8 * k:8 * k + 1] for k in range(S)]
        total_of = [cols[slots:2 * slots, 8 * k:8 * k + 1] for k in range(S)]
        top = peak_of[0]
        for k in range(1, S):
            top = jnp.maximum(top, peak_of[k])
        scale = [jnp.exp(p - top) for p in peak_of]
        denom = scale[0] * total_of[0]
        for k in range(1, S):
            denom = denom + scale[k] * total_of[k]
        for k in range(S):
            weight[i, k] = jnp.broadcast_to(scale[k] / denom, (slots, 128))
        arrive(rs)
        total = part_in[(i,) + mine].astype(F32) * weight[i, 0, mine[0]][:, 0:1]
        for k in range(1, S):
            total = total + rs_in[i, k - 1].astype(F32) * weight[i, k, mine[0]][:, 0:1]
        full_in[(i,) + mine] = total.astype(BF16)
        return gather(Z_INF, i, full_in)

    def dispatch(i):
        d = (prob[i] * weight[i, 0][:, 0:1]).astype(BF16)
        disp[i] = d
        for g in range(E):
            dsend[g, i * slots:(i + 1) * slots] = d[:, g * tl:(g + 1) * tl]

    def expert_forward(i):
        v = nn(full_in[i], win[0])
        half, slope = gelu_parts(v)
        value = (v * half).astype(BF16)
        act[i] = value
        pre[i] = half + slope
        return value

    def expert_out(i, value):
        part_out[i] = nn(value, wout[0]).astype(BF16)
        return scatter(Z_OUT, i, part_out, rs_out)

    def expert_backward(i):
        grad_pre = (nt(full_grad[i], wout[0]) * pre[i]).astype(BF16)
        gpre[i] = grad_pre
        part_gin[i] = nt(grad_pre, win[0]).astype(BF16)
        return scatter(Z_GIN, i, part_gin, rs_gin)

    colbuf[...] = jnp.zeros_like(colbuf)
    for i in range(images):
        statbuf[i, 8 * S:] = jnp.zeros_like(statbuf[i, 8 * S:])
    every_image = range(images)
    st, in_rs, grad_rs, in_ag, grad_ag = {}, {}, {}, {}, {}
    out_rs, gin_rs, out_ag, gin_ag = {}, {}, {}, {}
    emb_l.wait()
    emb_all[0] = emb[...]
    softmax(0)
    pl.semaphore_wait(barrier, S - 1 + E - 1)
    st[0], in_rs[0] = softmax_send(0)
    emb_ag = start([ecopy(E_EMB, k, emb_all.at[0], emb_all.at[k]) for k in range(1, E)])
    comb_l.wait()
    grad_rs[0] = out_grads(0)
    for i in range(1, images):
        softmax(i)
        st[i], in_rs[i] = softmax_send(i)
        in_ag[i - 1] = slot_inputs(i - 1, st[i - 1], in_rs[i - 1])
        grad_rs[i] = out_grads(i)
        dispatch(i - 1)
    last = images - 1
    in_ag[last] = slot_inputs(last, st[last], in_rs[last])
    dispatch(last)
    disp_all[0] = dsend[e]
    disp_a2a = start([ecopy(E_DISP, k, dsend.at[epeer[k]], disp_all.at[k]) for k in range(1, E)])
    for i in every_image:
        grad_ag[i] = sum_and_gather(grad_rs[i], Z_GRADF, i, part_grad, rs_grad, full_grad)

    win_l.wait()
    wout_l.wait()
    for i in every_image:
        arrive(in_ag[i])
        out_rs[i] = expert_out(i, expert_forward(i))
    stores.append(move(full_in, sin_h))
    stores.append(move(act, act_h))
    for i in every_image:
        arrive(grad_ag[i])
        gin_rs[i] = expert_backward(i)
        out_ag[i] = sum_and_gather(out_rs[i], Z_OUTF, i, part_out, rs_out, full_out)
    stores.append(move(full_grad, gso_h))
    stores.append(move(gpre, gpre_h))
    for i in every_image:
        gin_ag[i] = sum_and_gather(gin_rs[i], Z_GINF, i, part_gin, rs_gin, full_gin)

    per_row = 8 // images
    row_width = patches // per_row
    for i in every_image:
        arrive(out_ag[i])
        gc = nt(full_out[i], go[i])
        gcomb[i] = gc
        rd = jnp.sum(combt[i].astype(F32) * gc, axis=0, keepdims=True)
        for q in range(per_row):
            row_buf[0, i * per_row + q:i * per_row + q + 1] = rd[:, q * row_width:(q + 1) * row_width]
    row_x = start([ecopy(E_ROW, k, row_buf.at[0], row_buf.at[k]) for k in range(1, E)])

    direct = [1] + list(range(2, E, 2))
    gin_x, col_x = {}, {}
    for i in every_image:
        arrive(gin_ag[i])
        gin_all[i, 0] = full_gin[i]
        gin_x[i] = start([ecopy(E_GIN + i, k, gin_all.at[i, 0], gin_all.at[i, k]) for k in direct])
        gd = nt(full_gin[i], tok[i])
        gdisp[i] = gd
        cd = jnp.sum(disp[i].astype(F32) * gd, axis=1, keepdims=True)
        colbuf[0:slots] = jnp.broadcast_to(cd, (slots, 128))
        esend[i] = colbuf[...].T[0:8]
        col_x[i] = start([zcopy(Z_COL, i, k, esend.at[i], erecv.at[i, k - 1])
                          for k in range(1, S)])
    arrive(row_x)
    row_total = row_buf[0]
    for k in range(1, E):
        row_total = row_total + row_buf[k]
    for i in every_image:
        rd = jnp.concatenate(
            [row_total[i * per_row + q:i * per_row + q + 1] for q in range(per_row)], axis=1)
        gcomb[i] = combt[i].astype(F32) * (gcomb[i] - rd)
    grads = []
    for i in every_image:
        arrive(col_x[i])
        col_total = esend[i]
        for k in range(1, S):
            col_total = col_total + erecv[i, k - 1]
        colbuf[0:8] = col_total
        col_dot = colbuf[...].T[0:slots, 0:1]
        gl = (disp[i].astype(F32) * (gdisp[i] - col_dot) + gcomb[i]).astype(BF16)
        grads.append(gl)
        for g in range(E):
            lsend[g, i * slots:(i + 1) * slots] = gl[:, g * tl:(g + 1) * tl]
    log_all[0] = lsend[e]
    log_a2a = start([ecopy(E_LOG, k, lsend.at[epeer[k]], log_all.at[k]) for k in range(1, E)])
    embed_part = nn(grads[0], tok[0])
    for i in range(1, images):
        embed_part = embed_part + nn(grads[i], tok[i])
    embed_part = embed_part.astype(BF16)
    eo = width // S
    for g in range(S):
        embed_send[g] = embed_part[:, g * eo:(g + 1) * eo]
    embed_rs = start([zcopy(Z_EMB, 0, k, embed_send.at[zpeer[k]], embed_recv.at[k - 1])
                      for k in range(1, S)])

    forward = {}
    for i in every_image:
        forward[i] = []
        for n, k in enumerate(direct):
            gin_x[i][n].wait_recv()
            if k > 1:
                forward[i] += start([
                    ecopy(E_GIN + i, k + 1, gin_all.at[i, k], gin_all.at[i, k + 1], to=1)])
    arrive(disp_a2a)
    arrive(emb_ag)
    arrive(log_a2a)
    every = emb_all[...].reshape(E * slots, width)
    for i in every_image:
        here = slice(i * slots, (i + 1) * slots)
        total = tn(log_all[:, here].reshape(E * slots, tl), every)
        arrive(forward[i])
        total = total + tn(disp_all[:, here].reshape(E * slots, tl),
                           gin_all[i].reshape(E * slots, width))
        gt[i] = total.astype(BF16)
        stores.append(move(gt.at[i], gt_h.at[i]))
    arrive(embed_rs)
    total = embed_send[s].astype(F32)
    for k in range(1, S):
        total = total + embed_recv[k - 1].astype(F32)
    ge[...] = total.astype(BF16)
    stores.append(move(ge, ge_h))
    for c in sent:
        c.wait_send()
    for c in stores:
        c.wait()


def weights_kernel(steps, sin_h, gpre_h, act_h, gso_h, gt_h, ge_h,
                   gw_in_h, gw_out_h, gt_o, ge_o,
                   sin, gpre, act, gso, block_in, block_out, sems):
    images, slots, width = sin.shape
    rows = images * slots
    loads = [pltpu.make_async_copy(src, dst, sems.at[n]) for n, (src, dst) in enumerate(
        [(sin_h, sin), (gpre_h, gpre), (act_h, act), (gso_h, gso), (gt_h, gt_o), (ge_h, ge_o)])]
    for c in loads:
        c.start()
    n = len(loads)
    out = []
    for left_ref, right_ref, block, dst, first in (
            (sin, gpre, block_in, gw_in_h, 0), (act, gso, block_out, gw_out_h, 2)):
        loads[first].wait()
        loads[first + 1].wait()
        left = left_ref[...].reshape(rows, -1)
        right = right_ref[...].reshape(rows, -1)
        size = left.shape[1] // steps
        for b in range(steps):
            block[b] = tn(left[:, b * size:(b + 1) * size], right).astype(BF16)
            c = pltpu.make_async_copy(block.at[b], dst.at[0, pl.ds(b * size, size)], sems.at[n])
            n += 1
            c.start()
            out.append(c)
    for c in out + loads[4:]:
        c.wait()


def local(S, E, tokens, slot_embed, combine, w_in, w_out, grad_out):
    images, patches, width = tokens.shape
    slots = slot_embed.shape[1]
    hidden = w_in.shape[2]
    rows = images * slots
    own = rows // S
    tl = patches // E
    any_spec = pl.BlockSpec(memory_space=pl.ANY)
    vmem_spec = pl.BlockSpec(memory_space=pltpu.VMEM)

    def shape(*dims, dtype=BF16):
        return jax.ShapeDtypeStruct(dims, dtype)

    def vmem(*dims, dtype=BF16):
        return pltpu.VMEM(dims, dtype)

    flops = 2 * images * patches * slots * width * 7 + 8 * rows * width * hidden
    chunk = (images, S - 1, 16, slots * width // (16 * S))
    whole = (images, slots, width)
    inner = (images, slots, hidden)
    outs = (
        shape(images, tl, width), shape(slots, width // S), shape(*inner),
        shape(*whole), shape(*whole), shape(*inner),
    )
    gt, ge, act, gso, slot_in, gpre = pl.pallas_call(
        functools.partial(main_kernel, S, E),
        out_shape=outs,
        in_specs=[any_spec] * 6,
        out_specs=(any_spec,) * 6,
        scratch_shapes=[
            vmem(slots, width), vmem(*tokens.shape),
            vmem(*grad_out.shape), vmem(*w_in.shape), vmem(*w_out.shape),
            vmem(E, slots, width), vmem(E, rows, tl), vmem(images, E, slots, width),
            vmem(E, rows, tl), vmem(E, rows, tl), vmem(E, rows, tl),
            vmem(E, 8, images * patches // 8, dtype=F32),
            vmem(images, slots, patches, dtype=F32), vmem(images, slots, patches),
            vmem(images, slots, patches), vmem(images, slots, patches, dtype=F32),
            vmem(images, slots, patches, dtype=F32),
            vmem(images, S, slots, 128, dtype=F32), vmem(images, 128, 128, dtype=F32),
            vmem(128, 128, dtype=F32),
            vmem(*whole), vmem(*whole), vmem(*whole), vmem(*whole),
            vmem(*chunk), vmem(*chunk), vmem(*chunk), vmem(*chunk),
            vmem(*whole), vmem(*whole), vmem(*whole), vmem(*whole),
            vmem(*inner), vmem(*inner), vmem(images, tl, width), vmem(slots, width // S),
            vmem(*inner, dtype=F32),
            vmem(images, 8, 128, dtype=F32), vmem(images, S - 1, 8, 128, dtype=F32),
            vmem(S, slots, width // S), vmem(S - 1, slots, width // S),
            pltpu.SemaphoreType.DMA((Z_KINDS * images, S)),
            pltpu.SemaphoreType.DMA((Z_KINDS * images, S)),
            pltpu.SemaphoreType.DMA((E_GIN + images, E)),
            pltpu.SemaphoreType.DMA((E_GIN + images, E)),
            pltpu.SemaphoreType.DMA((9 + 3 * images,)),
        ],
        compiler_params=pltpu.CompilerParams(
            collective_id=0, has_side_effects=True, vmem_limit_bytes=56 * 2**20),
        cost_estimate=pl.CostEstimate(
            flops=flops, bytes_accessed=18 * 2**20, transcendentals=images * patches * slots),
        name="moe_backward",
    )(slot_embed.T, tokens, jnp.swapaxes(combine, 1, 2), grad_out, w_in, w_out)

    steps = 5 if width % (5 * 128) == 0 and hidden % (5 * 128) == 0 else 1
    gw_in, gw_out, gt, ge = pl.pallas_call(
        functools.partial(weights_kernel, steps),
        out_shape=(shape(1, width, hidden), shape(1, hidden, width)) + outs[:2],
        in_specs=[any_spec] * 6,
        out_specs=(any_spec,) * 4,
        scratch_shapes=[
            vmem(*whole), vmem(*inner), vmem(*inner), vmem(*whole),
            vmem(steps, width // steps, hidden), vmem(steps, hidden // steps, width),
            pltpu.SemaphoreType.DMA((6 + 2 * steps,)),
        ],
        compiler_params=pltpu.CompilerParams(vmem_limit_bytes=56 * 2**20),
        name="weight_gradients",
    )(slot_in, gpre, act, gso, gt, ge)
    return gt, ge.T, gw_in, gw_out


def solution(mesh):
    return jax.shard_map(
        functools.partial(local, mesh.shape["seq"], mesh.shape["expert"]),
        mesh=mesh,
        in_specs=(
            P(None, "seq", None),
            P(None, "expert"),
            P(None, "seq", "expert"),
            P("expert", None, "seq"),
            P("expert", "seq", None),
            P(None, "seq", None),
        ),
        out_specs=(
            P(None, ("seq", "expert"), None),
            P("seq", "expert"),
            P("expert", None, "seq"),
            P("expert", "seq", None),
        ),
        check_vma=False,
    )
```

```python
import functools
import math

import jax
import jax.numpy as jnp
from jax import lax
from jax.experimental import pallas as pl
from jax.experimental.pallas import tpu as pltpu
from jax.sharding import PartitionSpec as P

MESH = pl.DeviceIdType.MESH
BF16 = jnp.bfloat16
F32 = jnp.float32

Z_STAT, Z_IN, Z_GRAD, Z_OUT, Z_GIN, Z_COL, Z_KINDS = range(7)
G_IN, G_GRAD, G_OUT, G_GIN, G_EMB, G_KINDS = range(6)
E_EMB, E_COMB, E_DISP, E_ROW, E_LOG, E_GIN, E_KINDS = range(7)
LOCAL = 12


def nn(a, b):
    return lax.dot_general(a, b, (((1,), (0,)), ((), ())), preferred_element_type=F32)


def nt(a, b):
    return lax.dot_general(a, b, (((1,), (1,)), ((), ())), preferred_element_type=F32)


def tn(a, b):
    return lax.dot_general(a, b, (((0,), (0,)), ((), ())), preferred_element_type=F32)


def gelu_parts(v):
    half = 0.5 * (1.0 + lax.erf(v * (1.0 / math.sqrt(2.0))))
    return half, v * jnp.exp(-0.5 * v * v) * (1.0 / math.sqrt(2.0 * math.pi))


def flip(index, k):
    out = index
    bit = 1
    while bit <= k:
        if k & bit:
            out = out + bit * (1 - 2 * ((index // bit) % 2))
        bit *= 2
    return out


def main_kernel(
    S, E,
    emb_h, tok_h, comb_h, go_h, win_h, wout_h,
    gt_h, ge_h, act_h, gso_h, sin_h, gpre_h,
    tok, go, comb, win, wout,
    emb_all, disp_all, gin_all, log_all, dsend, lsend, row_buf,
    prob, disp, gcomb, weight, statbuf, colbuf,
    part_in, part_grad, part_out, part_gin,
    rs_in, rs_grad, rs_out, rs_gin,
    own_in, own_grad,
    full_in, full_grad, full_out, full_gin,
    act, gpre, gt, ge, esend, erecv, embed_send, embed_recv,
    zs, zr, gs, gr, es, er, ls,
):
    patches, width = tok.shape
    slots = comb.shape[1]
    rows = 2 * slots
    tl = patches // E
    chips = E // 2
    csplit = S // (slots // 16)
    cw = width // csplit
    s = lax.axis_index("seq")
    e = lax.axis_index("expert")
    c = e % 2
    zpeer = [flip(s, k) for k in range(S)]
    epeer = [flip(e, k) for k in range(E)]
    core = [c, 1 - c]

    local_copies = []

    def move(src, dst):
        copy = pltpu.make_async_copy(src, dst, ls.at[len(local_copies)])
        local_copies.append(copy)
        copy.start()
        return copy

    emb_l = move(emb_h, emb_all.at[0, c])
    tok_l = move(tok_h.at[c], tok)
    comb_l = move(comb_h.at[c], comb.at[c])
    go_l = move(go_h.at[c], go)
    win_l = move(win_h, win)
    wout_l = move(wout_h, wout)
    stores = []

    barrier = pltpu.get_barrier_semaphore()
    for k in range(1, E):
        pl.semaphore_signal(barrier, inc=1, device_id=(s, epeer[k]), device_id_type=MESH)
    for k in range(1, S):
        for kk in range(2):
            pl.semaphore_signal(
                barrier, inc=1, device_id=(zpeer[k], epeer[kk]), device_id_type=MESH)

    sent = []

    def zcopy(kind, k, src, dst):
        return pltpu.make_async_remote_copy(
            src_ref=src, dst_ref=dst, send_sem=zs.at[kind, k], recv_sem=zr.at[kind, k],
            device_id=(zpeer[k], e), device_id_type=MESH)

    def gcopy(kind, kk, k, src, dst):
        return pltpu.make_async_remote_copy(
            src_ref=src, dst_ref=dst, send_sem=gs.at[kind, kk * S + k],
            recv_sem=gr.at[kind, kk * S + k],
            device_id=(zpeer[k], epeer[kk]), device_id_type=MESH)

    def ecopy(kind, k, src, dst, to=None):
        return pltpu.make_async_remote_copy(
            src_ref=src, dst_ref=dst, send_sem=es.at[kind, k], recv_sem=er.at[kind, k],
            device_id=(s, epeer[k if to is None else to]), device_id_type=MESH)

    def start(group):
        for copy in group:
            copy.start()
        sent.extend(group)
        return group

    def arrive(group):
        for copy in group:
            copy.wait_recv()

    group = [(kk, k) for kk in range(2) for k in range(S) if (kk, k) != (0, 0)]

    def part_of(owner):
        return (pl.ds(pl.multiple_of((owner // csplit) * 16, 16), 16),
                pl.ds(pl.multiple_of((owner % csplit) * cw, 128), cw))

    parts = [part_of(p) for p in zpeer]
    mine = parts[0]
    pair = slice(None)

    def scatter_patches(kind, part, into):
        return start([zcopy(kind, k, part.at[(pair,) + parts[k]], into.at[k])
                      for k in range(1, S)])

    def gather_expert(kind, own, full):
        full[(c,) + mine] = own[c]
        return start([gcopy(kind, kk, k, own.at[core[kk]], full.at[(c,) + mine])
                      for kk, k in group])

    def scatter_expert(kind, part, into):
        into[0, c] = part[(c,) + mine]
        return start([gcopy(kind, kk, k, part.at[(core[kk],) + parts[k]], into.at[k, c])
                      for kk, k in group])

    def sum_and_gather(rs, kind, into, full):
        arrive(rs)
        total = into[0].astype(F32)
        for k in range(1, S):
            total = total + into[k].astype(F32)
        here = (pair,) + mine
        full[here] = total.astype(BF16)
        return start([zcopy(kind, k, full.at[here], full.at[here]) for k in range(1, S)])

    def both(ref):
        return ref[...].reshape(rows, ref.shape[-1])

    colbuf[...] = jnp.zeros_like(colbuf)
    statbuf[8 * S:] = jnp.zeros_like(statbuf[8 * S:])

    pl.semaphore_wait(barrier, E - 1 + 2 * (S - 1))
    emb_ag = start([ecopy(E_EMB, 1, emb_h, emb_all.at[0, c])])
    comb_x = start([ecopy(E_COMB, 1, comb_h.at[1 - c], comb.at[c])])
    emb_ag += start([ecopy(E_EMB, k, emb_h, emb_all.at[k // 2, c]) for k in range(2, E)])

    emb_l.wait()
    arrive(emb_ag[:1])
    tok_l.wait()
    logits = nt(emb_all[0].reshape(rows, width), tok[...])
    peak = jnp.max(logits, axis=1, keepdims=True)
    value = jnp.exp(logits - peak)
    prob[...] = value
    part_in[...] = nn(value.astype(BF16), tok[...]).astype(BF16).reshape(2, slots, width)
    in_rs = scatter_patches(Z_IN, part_in, rs_in)
    colbuf[0:rows] = jnp.broadcast_to(peak, (rows, 128))
    colbuf[rows:2 * rows] = jnp.broadcast_to(jnp.sum(value, axis=1, keepdims=True), (rows, 128))
    statbuf[0:8] = colbuf[...].T[0:8]
    stats = start([zcopy(Z_STAT, k, statbuf.at[pl.ds(0, 8)], statbuf.at[pl.ds(8 * k, 8)])
                   for k in range(1, S)])

    comb_l.wait()
    arrive(comb_x)
    go_l.wait()
    part_grad[...] = nn(both(comb), go[...]).astype(BF16).reshape(2, slots, width)
    grad_rs = scatter_patches(Z_GRAD, part_grad, rs_grad)

    arrive(stats)
    cols = statbuf[...].T
    peak_of = [cols[0:rows, 8 * k:8 * k + 1] for k in range(S)]
    total_of = [cols[rows:2 * rows, 8 * k:8 * k + 1] for k in range(S)]
    top = peak_of[0]
    for k in range(1, S):
        top = jnp.maximum(top, peak_of[k])
    scale = [jnp.exp(p - top) for p in peak_of]
    denom = scale[0] * total_of[0]
    for k in range(1, S):
        denom = denom + scale[k] * total_of[k]
    for k in range(S):
        weight[k] = jnp.broadcast_to(scale[k] / denom, (rows, 128)).reshape(2, slots, 128)
    d = (prob[...] * (scale[0] / denom)).astype(BF16)
    disp[...] = d
    arrive(in_rs)
    for x in range(2):
        total = part_in[(x,) + mine].astype(F32) * weight[0, x, mine[0]][:, 0:1]
        for k in range(1, S):
            total = total + rs_in[k, x].astype(F32) * weight[k, x, mine[0]][:, 0:1]
        own_in[x] = total.astype(BF16)
    in_ag = gather_expert(G_IN, own_in, full_in)

    for g in range(E):
        dsend[g] = d[:, g * tl:(g + 1) * tl]
    disp_all[c, 0] = dsend[e]
    disp_a2a = start([ecopy(E_DISP, k, dsend.at[epeer[k]], disp_all.at[c, k // 2])
                      for k in range(1, E)])

    arrive(grad_rs)
    for x in range(2):
        total = part_grad[(x,) + mine].astype(F32)
        for k in range(1, S):
            total = total + rs_grad[k, x].astype(F32)
        own_grad[x] = total.astype(BF16)
    grad_ag = gather_expert(G_GRAD, own_grad, full_grad)

    win_l.wait()
    arrive(in_ag)
    v = nn(both(full_in), win[0])
    half, slope = gelu_parts(v)
    a = (v * half).astype(BF16)
    act[...] = a.reshape(act.shape)
    slope = half + slope
    wout_l.wait()
    part_out[...] = nn(a, wout[0]).astype(BF16).reshape(2, slots, width)
    out_rs = scatter_expert(G_OUT, part_out, rs_out)
    stores.append(move(full_in, sin_h))
    stores.append(move(act, act_h))
    arrive(grad_ag)
    grad_pre = (nt(both(full_grad), wout[0]) * slope).astype(BF16)
    gpre[...] = grad_pre.reshape(gpre.shape)
    part_gin[...] = nt(grad_pre, win[0]).astype(BF16).reshape(2, slots, width)
    gin_rs = scatter_expert(G_GIN, part_gin, rs_gin)
    stores.append(move(full_grad, gso_h))
    stores.append(move(gpre, gpre_h))
    out_ag = sum_and_gather(out_rs, Z_OUT, rs_out, full_out)
    gin_ag = sum_and_gather(gin_rs, Z_GIN, rs_gin, full_gin)

    arrive(out_ag)
    gc = nt(both(full_out), go[...])
    gcomb[...] = gc
    rd = jnp.sum(both(comb).astype(F32) * gc, axis=0, keepdims=True)
    lanes = patches // 8
    for q in range(8):
        row_buf[0, q:q + 1] = rd[:, q * lanes:(q + 1) * lanes]
    row_x = start([ecopy(E_ROW, 2 * k, row_buf.at[0], row_buf.at[k]) for k in range(1, chips)])

    direct = [1] + list(range(2, E, 2))
    arrive(gin_ag)
    gin_all[c, 0] = full_gin[...]
    gin_x = start([ecopy(E_GIN, k, gin_all.at[c, 0], gin_all.at[c, k // 2]) for k in direct])
    gd = nt(both(full_gin), tok[...])
    cd = jnp.sum(disp[...].astype(F32) * gd, axis=1, keepdims=True)
    colbuf[0:rows] = jnp.broadcast_to(cd, (rows, 128))
    esend[...] = colbuf[...].T[0:8]
    col_x = start([zcopy(Z_COL, k, esend, erecv.at[k]) for k in range(1, S)])
    arrive(row_x)
    row_total = row_buf[0]
    for k in range(1, chips):
        row_total = row_total + row_buf[k]
    rd = jnp.concatenate([row_total[q:q + 1] for q in range(8)], axis=1)
    combine_term = both(comb).astype(F32) * (gcomb[...] - rd)
    arrive(col_x)
    col_total = esend[...]
    for k in range(1, S):
        col_total = col_total + erecv[k]
    colbuf[0:8] = col_total
    col_dot = colbuf[...].T[0:rows, 0:1]
    gl = (disp[...].astype(F32) * (gd - col_dot) + combine_term).astype(BF16)
    for g in range(E):
        lsend[g] = gl[:, g * tl:(g + 1) * tl]
    log_all[c, 0] = lsend[e]
    log_a2a = start([ecopy(E_LOG, k, lsend.at[epeer[k]], log_all.at[c, k // 2])
                     for k in range(1, E)])
    embed_part = nn(gl, tok[...]).astype(BF16)
    eo = width // S
    for g in range(S):
        for x in range(2):
            embed_send[g, x] = embed_part[x * slots:(x + 1) * slots, g * eo:(g + 1) * eo]
    embed_recv[0] = embed_send[s, c]
    embed_rs = start([gcopy(G_EMB, kk, k, embed_send.at[zpeer[k], core[kk]],
                            embed_recv.at[kk * S + k]) for kk, k in group])

    forward = []
    for copy, k in zip(gin_x, direct):
        copy.wait_recv()
        if k > 1:
            forward += start([
                ecopy(E_GIN, k + 1, gin_all.at[c, k // 2], gin_all.at[c, k // 2], to=1)])
    arrive(disp_a2a)
    arrive(emb_ag[1:])
    arrive(log_a2a)
    every = emb_all[...].reshape(chips * rows, width)
    for i in range(2):
        total = tn(log_all[i].reshape(chips * rows, tl), every)
        if i == 0:
            arrive(forward)
        total = total + tn(disp_all[i].reshape(chips * rows, tl),
                           gin_all[i].reshape(chips * rows, width))
        gt[i] = total.astype(BF16)
        stores.append(move(gt.at[i], gt_h.at[i]))
    arrive(embed_rs)
    total = embed_recv[0].astype(F32)
    for k in range(1, 2 * S):
        total = total + embed_recv[k].astype(F32)
    ge[...] = total.astype(BF16)
    stores.append(move(ge, ge_h))
    for copy in sent:
        copy.wait_send()
    for copy in stores:
        copy.wait()


def weights_kernel(steps, sin_h, gpre_h, act_h, gso_h, gt_h, ge_h,
                   gw_in_h, gw_out_h, gt_o, ge_o,
                   sin, gpre, act, gso, gt, ge, block_in, block_out, sems):
    images, slots, width = sin.shape
    rows = images * slots
    loads = [pltpu.make_async_copy(src, dst, sems.at[n]) for n, (src, dst) in enumerate(
        [(sin_h, sin), (gpre_h, gpre), (act_h, act), (gso_h, gso), (gt_h, gt), (ge_h, ge)])]
    for c in loads:
        c.start()
    n = len(loads)
    out = []
    for left_ref, right_ref, block, dst, first in (
            (sin, gpre, block_in, gw_in_h, 0), (act, gso, block_out, gw_out_h, 2)):
        loads[first].wait()
        loads[first + 1].wait()
        left = left_ref[...].reshape(rows, -1)
        right = right_ref[...].reshape(rows, -1)
        size = left.shape[1] // steps
        for b in range(steps):
            block[b] = tn(left[:, b * size:(b + 1) * size], right).astype(BF16)
            c = pltpu.make_async_copy(block.at[b], dst.at[0, pl.ds(b * size, size)], sems.at[n])
            n += 1
            c.start()
            out.append(c)
        if first == 0:
            for load, src, dst in ((loads[4], gt, gt_o), (loads[5], ge, ge_o)):
                load.wait()
                c = pltpu.make_async_copy(src, dst, sems.at[n])
                n += 1
                c.start()
                out.append(c)
    for c in out:
        c.wait()


def local(S, E, tokens, slot_embed, combine, w_in, w_out, grad_out):
    images, patches, width = tokens.shape
    assert images == 2 and w_in.shape[0] == 1 and E % 2 == 0
    slots = slot_embed.shape[1]
    hidden = w_in.shape[2]
    rows = images * slots
    tl = patches // E
    any_spec = pl.BlockSpec(memory_space=pl.ANY)
    vmem_spec = pl.BlockSpec(memory_space=pltpu.VMEM)

    def shape(*dims, dtype=BF16):
        return jax.ShapeDtypeStruct(dims, dtype)

    def vmem(*dims, dtype=BF16):
        return pltpu.VMEM(dims, dtype)

    flops = 2 * images * patches * slots * width * 7 + 8 * rows * width * hidden
    chunk = (2, 16, slots * width // (16 * S))
    whole = (images, slots, width)
    inner = (images, slots, hidden)
    outs = (
        shape(images, tl, width), shape(slots, width // S), shape(*inner),
        shape(*whole), shape(*whole), shape(*inner),
    )
    gt, ge, act, gso, slot_in, gpre = pl.pallas_call(
        functools.partial(main_kernel, S, E),
        out_shape=outs,
        in_specs=[any_spec] * 6,
        out_specs=(any_spec,) * 6,
        scratch_shapes=[
            vmem(patches, width), vmem(patches, width), vmem(2, slots, patches),
            vmem(*w_in.shape), vmem(*w_out.shape),
            vmem(E // 2, 2, slots, width), vmem(2, E // 2, rows, tl),
            vmem(2, E // 2, 2, slots, width), vmem(2, E // 2, rows, tl),
            vmem(E, rows, tl), vmem(E, rows, tl), vmem(E // 2, 8, patches // 8, dtype=F32),
            vmem(rows, patches, dtype=F32), vmem(rows, patches), vmem(rows, patches, dtype=F32),
            vmem(S, 2, slots, 128, dtype=F32), vmem(128, 128, dtype=F32),
            vmem(128, 128, dtype=F32),
            vmem(*whole), vmem(*whole), vmem(*whole), vmem(*whole),
            vmem(S, *chunk), vmem(S, *chunk), vmem(S, *chunk), vmem(S, *chunk),
            vmem(*chunk), vmem(*chunk),
            vmem(*whole), vmem(*whole), vmem(*whole), vmem(*whole),
            vmem(*inner), vmem(*inner), vmem(images, tl, width), vmem(slots, width // S),
            vmem(8, 128, dtype=F32), vmem(S, 8, 128, dtype=F32),
            vmem(S, 2, slots, width // S), vmem(2 * S, slots, width // S),
            pltpu.SemaphoreType.DMA((Z_KINDS, S)), pltpu.SemaphoreType.DMA((Z_KINDS, S)),
            pltpu.SemaphoreType.DMA((G_KINDS, 2 * S)), pltpu.SemaphoreType.DMA((G_KINDS, 2 * S)),
            pltpu.SemaphoreType.DMA((E_KINDS, E)), pltpu.SemaphoreType.DMA((E_KINDS, E)),
            pltpu.SemaphoreType.DMA((LOCAL + 2,)),
        ],
        compiler_params=pltpu.CompilerParams(
            collective_id=0, has_side_effects=True, vmem_limit_bytes=56 * 2**20),
        cost_estimate=pl.CostEstimate(
            flops=flops, bytes_accessed=18 * 2**20, transcendentals=images * patches * slots),
        name="moe_backward",
    )(slot_embed.T, tokens, jnp.swapaxes(combine, 1, 2), grad_out, w_in, w_out)

    steps = 5 if width % (5 * 128) == 0 and hidden % (5 * 128) == 0 else 1
    gw_in, gw_out, gt, ge = pl.pallas_call(
        functools.partial(weights_kernel, steps),
        out_shape=(shape(1, width, hidden), shape(1, hidden, width)) + outs[:2],
        in_specs=[any_spec] * 6,
        out_specs=(any_spec,) * 4,
        scratch_shapes=[
            vmem(*whole), vmem(*inner), vmem(*inner), vmem(*whole),
            vmem(*outs[0].shape), vmem(*outs[1].shape),
            vmem(steps, width // steps, hidden), vmem(steps, hidden // steps, width),
            pltpu.SemaphoreType.DMA((8 + 2 * steps,)),
        ],
        compiler_params=pltpu.CompilerParams(vmem_limit_bytes=56 * 2**20),
        name="weight_gradients",
    )(slot_in, gpre, act, gso, gt, ge)
    return gt, ge.T, gw_in, gw_out


def solution(mesh):
    return jax.shard_map(
        functools.partial(local, mesh.shape["seq"], mesh.shape["expert"]),
        mesh=mesh,
        in_specs=(
            P(None, "seq", None),
            P(None, "expert"),
            P(None, "seq", "expert"),
            P("expert", None, "seq"),
            P("expert", "seq", None),
            P(None, "seq", None),
        ),
        out_specs=(
            P(None, ("seq", "expert"), None),
            P("seq", "expert"),
            P("expert", None, "seq"),
            P("expert", "seq", None),
        ),
        check_vma=False,
    )
```

```python
import functools
import math

import jax
import jax.numpy as jnp
from jax import lax
from jax.experimental import pallas as pl
from jax.experimental.pallas import tpu as pltpu
from jax.sharding import PartitionSpec as P

MESH = pl.DeviceIdType.MESH
BF16 = jnp.bfloat16
F32 = jnp.float32

(Z_STAT, Z_IN, Z_INF, Z_GRAD, Z_GRADF, Z_OUT, Z_OUTF, Z_GIN, Z_GINF, Z_COL, Z_EMB,
 Z_KINDS) = range(12)
E_EMB, E_DISP, E_ROW, E_LOG, E_GIN = range(5)


def nn(a, b):
    return lax.dot_general(a, b, (((1,), (0,)), ((), ())), preferred_element_type=F32)


def nt(a, b):
    return lax.dot_general(a, b, (((1,), (1,)), ((), ())), preferred_element_type=F32)


def tn(a, b):
    return lax.dot_general(a, b, (((0,), (0,)), ((), ())), preferred_element_type=F32)


def gelu_parts(v):
    half = 0.5 * (1.0 + lax.erf(v * (1.0 / math.sqrt(2.0))))
    return half, v * jnp.exp(-0.5 * v * v) * (1.0 / math.sqrt(2.0 * math.pi))


def flip(index, k):
    out = index
    bit = 1
    while bit <= k:
        if k & bit:
            out = out + bit * (1 - 2 * ((index // bit) % 2))
        bit *= 2
    return out


def main_kernel(
    S, E,
    emb_h, tok_h, comb_h, go_h, win_h, wout_h,
    gt_h, ge_h, act_h, gso_h, sin_h, gpre_h,
    emb, tok, go, win, wout,
    emb_all, disp_all, gin_all, log_all, dsend, lsend, row_buf,
    prob, disp, combt, gcomb, gdisp, weight, statbuf, colbuf,
    part_in, part_grad, part_out, part_gin,
    rs_in, rs_grad, rs_out, rs_gin,
    full_in, full_grad, full_out, full_gin,
    act, gpre, gt, ge, pre, esend, erecv, embed_send, embed_recv,
    zs, zr, es, er, ls,
):
    images, patches, width = tok.shape
    slots = combt.shape[1]
    tl = patches // E
    rsplit = slots // 16
    csplit = S // rsplit
    cw = width // csplit
    s = lax.axis_index("seq")
    e = lax.axis_index("expert")
    zpeer = [flip(s, k) for k in range(S)]
    epeer = [flip(e, k) for k in range(E)]

    local_copies = []

    def move(src, dst):
        c = pltpu.make_async_copy(src, dst, ls.at[len(local_copies)])
        local_copies.append(c)
        c.start()
        return c

    emb_l = move(emb_h, emb)
    tok_l = [move(tok_h.at[0], tok.at[0])]
    comb_l = move(comb_h, combt)
    go_l = [move(go_h.at[0], go.at[0])]
    for i in range(1, images):
        tok_l.append(move(tok_h.at[i], tok.at[i]))
        go_l.append(move(go_h.at[i], go.at[i]))
    win_l = move(win_h, win)
    wout_l = move(wout_h, wout)
    stores = []

    barrier = pltpu.get_barrier_semaphore()
    for k in range(1, S):
        pl.semaphore_signal(barrier, inc=1, device_id=(zpeer[k], e), device_id_type=MESH)
    for k in range(1, E):
        pl.semaphore_signal(barrier, inc=1, device_id=(s, epeer[k]), device_id_type=MESH)

    sent = []

    def zcopy(kind, i, k, src, dst):
        return pltpu.make_async_remote_copy(
            src_ref=src, dst_ref=dst, send_sem=zs.at[kind * images + i, k],
            recv_sem=zr.at[kind * images + i, k],
            device_id=(zpeer[k], e), device_id_type=MESH)

    def ecopy(kind, k, src, dst, to=None):
        return pltpu.make_async_remote_copy(
            src_ref=src, dst_ref=dst, send_sem=es.at[kind, k], recv_sem=er.at[kind, k],
            device_id=(s, epeer[k if to is None else to]), device_id_type=MESH)

    def start(group):
        for c in group:
            c.start()
        sent.extend(group)
        return group

    def arrive(group):
        for c in group:
            c.wait_recv()

    def part_of(owner):
        return (pl.ds(pl.multiple_of((owner // csplit) * 16, 16), 16),
                pl.ds(pl.multiple_of((owner % csplit) * cw, 128), cw))

    mine = part_of(s)
    theirs = [part_of(p) for p in zpeer]

    def scatter(kind, i, part, into):
        return start([zcopy(kind, i, k, part.at[(i,) + theirs[k]], into.at[i, k - 1])
                      for k in range(1, S)])

    def gather(kind, i, full):
        here = (i,) + mine
        return start([zcopy(kind, i, k, full.at[here], full.at[here]) for k in range(1, S)])

    def sum_and_gather(rs, kind, i, part, into, full):
        arrive(rs)
        here = (i,) + mine
        total = part[here].astype(F32)
        for k in range(1, S):
            total = total + into[i, k - 1].astype(F32)
        full[here] = total.astype(BF16)
        return gather(kind, i, full)

    def softmax(i):
        tok_l[i].wait()
        logits = nt(emb[...], tok[i])
        peak = jnp.max(logits, axis=1, keepdims=True)
        value = jnp.exp(logits - peak)
        prob[i] = value
        part_in[i] = nn(value.astype(BF16), tok[i]).astype(BF16)
        colbuf[0:slots] = jnp.broadcast_to(peak, (slots, 128))
        colbuf[slots:2 * slots] = jnp.broadcast_to(
            jnp.sum(value, axis=1, keepdims=True), (slots, 128))
        statbuf[i, 0:8] = colbuf[...].T[0:8]

    def softmax_send(i):
        st = start([zcopy(Z_STAT, i, k, statbuf.at[i, pl.ds(0, 8)],
                          statbuf.at[i, pl.ds(8 * k, 8)]) for k in range(1, S)])
        return st, scatter(Z_IN, i, part_in, rs_in)

    def out_grads(i):
        go_l[i].wait()
        part_grad[i] = nn(combt[i], go[i]).astype(BF16)
        return scatter(Z_GRAD, i, part_grad, rs_grad)

    def slot_inputs(i, st, rs):
        arrive(st)
        cols = statbuf[i].T
        peak_of = [cols[0:slots, 8 * k:8 * k + 1] for k in range(S)]
        total_of = [cols[slots:2 * slots, 8 * k:8 * k + 1] for k in range(S)]
        top = peak_of[0]
        for k in range(1, S):
            top = jnp.maximum(top, peak_of[k])
        scale = [jnp.exp(p - top) for p in peak_of]
        denom = scale[0] * total_of[0]
        for k in range(1, S):
            denom = denom + scale[k] * total_of[k]
        for k in range(S):
            weight[i, k] = jnp.broadcast_to(scale[k] / denom, (slots, 128))
        arrive(rs)
        total = part_in[(i,) + mine].astype(F32) * weight[i, 0, mine[0]][:, 0:1]
        for k in range(1, S):
            total = total + rs_in[i, k - 1].astype(F32) * weight[i, k, mine[0]][:, 0:1]
        full_in[(i,) + mine] = total.astype(BF16)
        return gather(Z_INF, i, full_in)

    def dispatch(i):
        d = (prob[i] * weight[i, 0][:, 0:1]).astype(BF16)
        disp[i] = d
        for g in range(E):
            dsend[g, i * slots:(i + 1) * slots] = d[:, g * tl:(g + 1) * tl]

    def expert_forward(i):
        v = nn(full_in[i], win[0])
        half, slope = gelu_parts(v)
        value = (v * half).astype(BF16)
        act[i] = value
        pre[i] = half + slope
        return value

    def expert_out(i, value):
        part_out[i] = nn(value, wout[0]).astype(BF16)
        return scatter(Z_OUT, i, part_out, rs_out)

    def every(ref):
        return ref[...].reshape(images * slots, ref.shape[-1])

    def expert_backward():
        grad_pre = (nt(every(full_grad), wout[0]) * every(pre)).astype(BF16)
        gpre[...] = grad_pre.reshape(gpre.shape)
        part_gin[...] = nt(grad_pre, win[0]).astype(BF16).reshape(part_gin.shape)

    colbuf[...] = jnp.zeros_like(colbuf)
    for i in range(images):
        statbuf[i, 8 * S:] = jnp.zeros_like(statbuf[i, 8 * S:])
    every_image = range(images)
    st, in_rs, grad_rs, in_ag, grad_ag = {}, {}, {}, {}, {}
    out_rs, gin_rs, out_ag, gin_ag = {}, {}, {}, {}
    emb_l.wait()
    emb_all[0] = emb[...]
    softmax(0)
    pl.semaphore_wait(barrier, S - 1 + E - 1)
    st[0], in_rs[0] = softmax_send(0)
    emb_ag = start([ecopy(E_EMB, k, emb_all.at[0], emb_all.at[k]) for k in range(1, E)])
    comb_l.wait()
    grad_rs[0] = out_grads(0)
    for i in range(1, images):
        softmax(i)
        st[i], in_rs[i] = softmax_send(i)
        in_ag[i - 1] = slot_inputs(i - 1, st[i - 1], in_rs[i - 1])
        grad_rs[i] = out_grads(i)
        dispatch(i - 1)
    last = images - 1
    in_ag[last] = slot_inputs(last, st[last], in_rs[last])
    dispatch(last)
    disp_all[0] = dsend[e]
    disp_a2a = start([ecopy(E_DISP, k, dsend.at[epeer[k]], disp_all.at[k]) for k in range(1, E)])
    for i in every_image:
        grad_ag[i] = sum_and_gather(grad_rs[i], Z_GRADF, i, part_grad, rs_grad, full_grad)

    win_l.wait()
    wout_l.wait()
    for i in every_image:
        arrive(in_ag[i])
        out_rs[i] = expert_out(i, expert_forward(i))
    stores.append(move(full_in, sin_h))
    stores.append(move(act, act_h))
    for i in every_image:
        arrive(grad_ag[i])
    expert_backward()
    for i in every_image:
        gin_rs[i] = scatter(Z_GIN, i, part_gin, rs_gin)
    for i in every_image:
        out_ag[i] = sum_and_gather(out_rs[i], Z_OUTF, i, part_out, rs_out, full_out)
    stores.append(move(full_grad, gso_h))
    stores.append(move(gpre, gpre_h))
    for i in every_image:
        gin_ag[i] = sum_and_gather(gin_rs[i], Z_GINF, i, part_gin, rs_gin, full_gin)

    per_row = 8 // images
    row_width = patches // per_row
    for i in every_image:
        arrive(out_ag[i])
        gc = nt(full_out[i], go[i])
        gcomb[i] = gc
        rd = jnp.sum(combt[i].astype(F32) * gc, axis=0, keepdims=True)
        for q in range(per_row):
            row_buf[0, i * per_row + q:i * per_row + q + 1] = rd[:, q * row_width:(q + 1) * row_width]
    row_x = start([ecopy(E_ROW, k, row_buf.at[0], row_buf.at[k]) for k in range(1, E)])

    direct = [1] + list(range(2, E, 2))
    gin_x, col_x = {}, {}
    for i in every_image:
        arrive(gin_ag[i])
        gin_all[i, 0] = full_gin[i]
        gin_x[i] = start([ecopy(E_GIN + i, k, gin_all.at[i, 0], gin_all.at[i, k]) for k in direct])
        gd = nt(full_gin[i], tok[i])
        gdisp[i] = gd
        cd = jnp.sum(disp[i].astype(F32) * gd, axis=1, keepdims=True)
        colbuf[0:slots] = jnp.broadcast_to(cd, (slots, 128))
        esend[i] = colbuf[...].T[0:8]
        col_x[i] = start([zcopy(Z_COL, i, k, esend.at[i], erecv.at[i, k - 1])
                          for k in range(1, S)])
    arrive(row_x)
    row_total = row_buf[0]
    for k in range(1, E):
        row_total = row_total + row_buf[k]
    for i in every_image:
        rd = jnp.concatenate(
            [row_total[i * per_row + q:i * per_row + q + 1] for q in range(per_row)], axis=1)
        gcomb[i] = combt[i].astype(F32) * (gcomb[i] - rd)
    grads = []
    for i in every_image:
        arrive(col_x[i])
        col_total = esend[i]
        for k in range(1, S):
            col_total = col_total + erecv[i, k - 1]
        colbuf[0:8] = col_total
        col_dot = colbuf[...].T[0:slots, 0:1]
        gl = (disp[i].astype(F32) * (gdisp[i] - col_dot) + gcomb[i]).astype(BF16)
        grads.append(gl)
        for g in range(E):
            lsend[g, i * slots:(i + 1) * slots] = gl[:, g * tl:(g + 1) * tl]
    log_all[0] = lsend[e]
    log_a2a = start([ecopy(E_LOG, k, lsend.at[epeer[k]], log_all.at[k]) for k in range(1, E)])
    embed_part = nn(grads[0], tok[0])
    for i in range(1, images):
        embed_part = embed_part + nn(grads[i], tok[i])
    embed_part = embed_part.astype(BF16)
    eo = width // S
    for g in range(S):
        embed_send[g] = embed_part[:, g * eo:(g + 1) * eo]
    embed_rs = start([zcopy(Z_EMB, 0, k, embed_send.at[zpeer[k]], embed_recv.at[k - 1])
                      for k in range(1, S)])

    forward = {}
    for i in every_image:
        forward[i] = []
        for n, k in enumerate(direct):
            gin_x[i][n].wait_recv()
            if k > 1:
                forward[i] += start([
                    ecopy(E_GIN + i, k + 1, gin_all.at[i, k], gin_all.at[i, k + 1], to=1)])
    arrive(disp_a2a)
    arrive(emb_ag)
    arrive(log_a2a)
    every_emb = emb_all[...].reshape(E * slots, width)
    for i in every_image:
        here = slice(i * slots, (i + 1) * slots)
        total = tn(log_all[:, here].reshape(E * slots, tl), every_emb)
        arrive(forward[i])
        total = total + tn(disp_all[:, here].reshape(E * slots, tl),
                           gin_all[i].reshape(E * slots, width))
        gt[i] = total.astype(BF16)
        stores.append(move(gt.at[i], gt_h.at[i]))
    arrive(embed_rs)
    total = embed_send[s].astype(F32)
    for k in range(1, S):
        total = total + embed_recv[k - 1].astype(F32)
    ge[...] = total.astype(BF16)
    stores.append(move(ge, ge_h))
    for c in sent:
        c.wait_send()
    for c in stores:
        c.wait()


def weights_kernel(steps, sin_h, gpre_h, act_h, gso_h, gt_h, ge_h,
                   gw_in_h, gw_out_h, gt_o, ge_o,
                   sin, gpre, act, gso, gt, ge, block_in, block_out, sems):
    images, slots, width = sin.shape
    rows = images * slots
    loads = [pltpu.make_async_copy(src, dst, sems.at[n]) for n, (src, dst) in enumerate(
        [(sin_h, sin), (gpre_h, gpre), (act_h, act), (gso_h, gso), (gt_h, gt), (ge_h, ge)])]
    for c in loads:
        c.start()
    n = len(loads)
    out = []
    for left_ref, right_ref, block, dst, first in (
            (sin, gpre, block_in, gw_in_h, 0), (act, gso, block_out, gw_out_h, 2)):
        loads[first].wait()
        loads[first + 1].wait()
        left = left_ref[...].reshape(rows, -1)
        right = right_ref[...].reshape(rows, -1)
        size = left.shape[1] // steps
        for b in range(steps):
            block[b] = tn(left[:, b * size:(b + 1) * size], right).astype(BF16)
            c = pltpu.make_async_copy(block.at[b], dst.at[0, pl.ds(b * size, size)], sems.at[n])
            n += 1
            c.start()
            out.append(c)
        if first == 0:
            for load, src, dst in ((loads[4], gt, gt_o), (loads[5], ge, ge_o)):
                load.wait()
                c = pltpu.make_async_copy(src, dst, sems.at[n])
                n += 1
                c.start()
                out.append(c)
    for c in out:
        c.wait()


def local(S, E, tokens, slot_embed, combine, w_in, w_out, grad_out):
    images, patches, width = tokens.shape
    slots = slot_embed.shape[1]
    hidden = w_in.shape[2]
    rows = images * slots
    own = rows // S
    tl = patches // E
    any_spec = pl.BlockSpec(memory_space=pl.ANY)
    vmem_spec = pl.BlockSpec(memory_space=pltpu.VMEM)

    def shape(*dims, dtype=BF16):
        return jax.ShapeDtypeStruct(dims, dtype)

    def vmem(*dims, dtype=BF16):
        return pltpu.VMEM(dims, dtype)

    flops = 2 * images * patches * slots * width * 7 + 8 * rows * width * hidden
    chunk = (images, S - 1, 16, slots * width // (16 * S))
    whole = (images, slots, width)
    inner = (images, slots, hidden)
    outs = (
        shape(images, tl, width), shape(slots, width // S), shape(*inner),
        shape(*whole), shape(*whole), shape(*inner),
    )
    gt, ge, act, gso, slot_in, gpre = pl.pallas_call(
        functools.partial(main_kernel, S, E),
        out_shape=outs,
        in_specs=[any_spec] * 6,
        out_specs=(any_spec,) * 6,
        scratch_shapes=[
            vmem(slots, width), vmem(*tokens.shape),
            vmem(*grad_out.shape), vmem(*w_in.shape), vmem(*w_out.shape),
            vmem(E, slots, width), vmem(E, rows, tl), vmem(images, E, slots, width),
            vmem(E, rows, tl), vmem(E, rows, tl), vmem(E, rows, tl),
            vmem(E, 8, images * patches // 8, dtype=F32),
            vmem(images, slots, patches, dtype=F32), vmem(images, slots, patches),
            vmem(images, slots, patches), vmem(images, slots, patches, dtype=F32),
            vmem(images, slots, patches, dtype=F32),
            vmem(images, S, slots, 128, dtype=F32), vmem(images, 128, 128, dtype=F32),
            vmem(128, 128, dtype=F32),
            vmem(*whole), vmem(*whole), vmem(*whole), vmem(*whole),
            vmem(*chunk), vmem(*chunk), vmem(*chunk), vmem(*chunk),
            vmem(*whole), vmem(*whole), vmem(*whole), vmem(*whole),
            vmem(*inner), vmem(*inner), vmem(images, tl, width), vmem(slots, width // S),
            vmem(*inner, dtype=F32),
            vmem(images, 8, 128, dtype=F32), vmem(images, S - 1, 8, 128, dtype=F32),
            vmem(S, slots, width // S), vmem(S - 1, slots, width // S),
            pltpu.SemaphoreType.DMA((Z_KINDS * images, S)),
            pltpu.SemaphoreType.DMA((Z_KINDS * images, S)),
            pltpu.SemaphoreType.DMA((E_GIN + images, E)),
            pltpu.SemaphoreType.DMA((E_GIN + images, E)),
            pltpu.SemaphoreType.DMA((9 + 3 * images,)),
        ],
        compiler_params=pltpu.CompilerParams(
            collective_id=0, has_side_effects=True, vmem_limit_bytes=56 * 2**20),
        cost_estimate=pl.CostEstimate(
            flops=flops, bytes_accessed=18 * 2**20, transcendentals=images * patches * slots),
        name="moe_backward",
    )(slot_embed.T, tokens, jnp.swapaxes(combine, 1, 2), grad_out, w_in, w_out)

    steps = 5 if width % (5 * 128) == 0 and hidden % (5 * 128) == 0 else 1
    gw_in, gw_out, gt, ge = pl.pallas_call(
        functools.partial(weights_kernel, steps),
        out_shape=(shape(1, width, hidden), shape(1, hidden, width)) + outs[:2],
        in_specs=[any_spec] * 6,
        out_specs=(any_spec,) * 4,
        scratch_shapes=[
            vmem(*whole), vmem(*inner), vmem(*inner), vmem(*whole),
            vmem(*outs[0].shape), vmem(*outs[1].shape),
            vmem(steps, width // steps, hidden), vmem(steps, hidden // steps, width),
            pltpu.SemaphoreType.DMA((8 + 2 * steps,)),
        ],
        compiler_params=pltpu.CompilerParams(vmem_limit_bytes=56 * 2**20),
        name="weight_gradients",
    )(slot_in, gpre, act, gso, gt, ge)
    return gt, ge.T, gw_in, gw_out


def solution(mesh):
    return jax.shard_map(
        functools.partial(local, mesh.shape["seq"], mesh.shape["expert"]),
        mesh=mesh,
        in_specs=(
            P(None, "seq", None),
            P(None, "expert"),
            P(None, "seq", "expert"),
            P("expert", None, "seq"),
            P("expert", "seq", None),
            P(None, "seq", None),
        ),
        out_specs=(
            P(None, ("seq", "expert"), None),
            P("seq", "expert"),
            P("expert", None, "seq"),
            P("expert", "seq", None),
        ),
        check_vma=False,
    )
```

```python
import functools
import math

import jax
import jax.numpy as jnp
from jax import lax
from jax.experimental import pallas as pl
from jax.experimental.pallas import tpu as pltpu
from jax.sharding import PartitionSpec as P

MESH = pl.DeviceIdType.MESH
BF16 = jnp.bfloat16
F32 = jnp.float32

(Z_STAT, Z_IN, Z_INF, Z_GRAD, Z_GRADF, Z_OUT, Z_OUTF, Z_GIN, Z_GINF, Z_COL, Z_EMB,
 Z_KINDS) = range(12)
E_EMB, E_DISP, E_ROW, E_LOG, E_GIN = range(5)


def nn(a, b):
    return lax.dot_general(a, b, (((1,), (0,)), ((), ())), preferred_element_type=F32)


def nt(a, b):
    return lax.dot_general(a, b, (((1,), (1,)), ((), ())), preferred_element_type=F32)


def tn(a, b):
    return lax.dot_general(a, b, (((0,), (0,)), ((), ())), preferred_element_type=F32)


def gelu_parts(v):
    half = 0.5 * (1.0 + lax.erf(v * (1.0 / math.sqrt(2.0))))
    return half, v * jnp.exp(-0.5 * v * v) * (1.0 / math.sqrt(2.0 * math.pi))


def flip(index, k):
    out = index
    bit = 1
    while bit <= k:
        if k & bit:
            out = out + bit * (1 - 2 * ((index // bit) % 2))
        bit *= 2
    return out


def main_kernel(
    S, E,
    emb_h, tok_h, comb_h, go_h, win_h, wout_h,
    gt_h, ge_h, act_h, gso_h, sin_h, gpre_h,
    emb, tok, go, win, wout,
    emb_all, disp_all, gin_all, log_all, dsend, lsend, row_buf,
    prob, disp, combt, gcomb, gdisp, weight, statbuf, colbuf,
    part_in, part_grad, part_out, part_gin,
    rs_in, rs_grad, rs_out, rs_gin,
    full_in, full_grad, full_out, full_gin,
    act, gpre, gt, ge, pre, esend, erecv, embed_send, embed_recv,
    zs, zr, es, er, ls,
):
    images, patches, width = tok.shape
    slots = combt.shape[1]
    tl = patches // E
    rsplit = slots // 16
    csplit = S // rsplit
    cw = width // csplit
    s = lax.axis_index("seq")
    e = lax.axis_index("expert")
    zpeer = [flip(s, k) for k in range(S)]
    epeer = [flip(e, k) for k in range(E)]

    local_copies = []

    def move(src, dst):
        c = pltpu.make_async_copy(src, dst, ls.at[len(local_copies)])
        local_copies.append(c)
        c.start()
        return c

    emb_l = move(emb_h, emb)
    tok_l = [move(tok_h.at[0], tok.at[0])]
    comb_l = move(comb_h, combt)
    go_l = [move(go_h.at[0], go.at[0])]
    for i in range(1, images):
        tok_l.append(move(tok_h.at[i], tok.at[i]))
        go_l.append(move(go_h.at[i], go.at[i]))
    win_l = move(win_h, win)
    wout_l = move(wout_h, wout)
    stores = []

    barrier = pltpu.get_barrier_semaphore()
    for k in range(1, S):
        pl.semaphore_signal(barrier, inc=1, device_id=(zpeer[k], e), device_id_type=MESH)
    for k in range(1, E):
        pl.semaphore_signal(barrier, inc=1, device_id=(s, epeer[k]), device_id_type=MESH)

    sent = []

    def zcopy(kind, i, k, src, dst):
        return pltpu.make_async_remote_copy(
            src_ref=src, dst_ref=dst, send_sem=zs.at[kind * images + i, k],
            recv_sem=zr.at[kind * images + i, k],
            device_id=(zpeer[k], e), device_id_type=MESH)

    def ecopy(kind, k, src, dst, to=None):
        return pltpu.make_async_remote_copy(
            src_ref=src, dst_ref=dst, send_sem=es.at[kind, k], recv_sem=er.at[kind, k],
            device_id=(s, epeer[k if to is None else to]), device_id_type=MESH)

    def start(group):
        for c in group:
            c.start()
        sent.extend(group)
        return group

    def arrive(group):
        for c in group:
            c.wait_recv()

    def part_of(owner):
        return (pl.ds(pl.multiple_of((owner // csplit) * 16, 16), 16),
                pl.ds(pl.multiple_of((owner % csplit) * cw, 128), cw))

    mine = part_of(s)
    theirs = [part_of(p) for p in zpeer]

    def scatter(kind, i, part, into):
        return start([zcopy(kind, i, k, part.at[(i,) + theirs[k]], into.at[i, k - 1])
                      for k in range(1, S)])

    def gather(kind, i, full):
        here = (i,) + mine
        return start([zcopy(kind, i, k, full.at[here], full.at[here]) for k in range(1, S)])

    def sum_and_gather(rs, kind, i, part, into, full):
        arrive(rs)
        here = (i,) + mine
        total = part[here].astype(F32)
        for k in range(1, S):
            total = total + into[i, k - 1].astype(F32)
        full[here] = total.astype(BF16)
        return gather(kind, i, full)

    def softmax(i):
        tok_l[i].wait()
        logits = nt(emb[...], tok[i])
        peak = jnp.max(logits, axis=1, keepdims=True)
        value = jnp.exp(logits - peak)
        prob[i] = value
        part_in[i] = nn(value.astype(BF16), tok[i]).astype(BF16)
        colbuf[0:slots] = jnp.broadcast_to(peak, (slots, 128))
        colbuf[slots:2 * slots] = jnp.broadcast_to(
            jnp.sum(value, axis=1, keepdims=True), (slots, 128))
        statbuf[i, 0:8] = colbuf[...].T[0:8]

    def softmax_send(i):
        st = start([zcopy(Z_STAT, i, k, statbuf.at[i, pl.ds(0, 8)],
                          statbuf.at[i, pl.ds(8 * k, 8)]) for k in range(1, S)])
        return st, scatter(Z_IN, i, part_in, rs_in)

    def out_grads(i):
        go_l[i].wait()
        part_grad[i] = nn(combt[i], go[i]).astype(BF16)
        return scatter(Z_GRAD, i, part_grad, rs_grad)

    def slot_inputs(i, st, rs):
        arrive(st)
        cols = statbuf[i].T
        peak_of = [cols[0:slots, 8 * k:8 * k + 1] for k in range(S)]
        total_of = [cols[slots:2 * slots, 8 * k:8 * k + 1] for k in range(S)]
        top = peak_of[0]
        for k in range(1, S):
            top = jnp.maximum(top, peak_of[k])
        scale = [jnp.exp(p - top) for p in peak_of]
        denom = scale[0] * total_of[0]
        for k in range(1, S):
            denom = denom + scale[k] * total_of[k]
        for k in range(S):
            weight[i, k] = jnp.broadcast_to(scale[k] / denom, (slots, 128))
        arrive(rs)
        total = part_in[(i,) + mine].astype(F32) * weight[i, 0, mine[0]][:, 0:1]
        for k in range(1, S):
            total = total + rs_in[i, k - 1].astype(F32) * weight[i, k, mine[0]][:, 0:1]
        full_in[(i,) + mine] = total.astype(BF16)
        return gather(Z_INF, i, full_in)

    def dispatch(i):
        d = (prob[i] * weight[i, 0][:, 0:1]).astype(BF16)
        disp[i] = d
        for g in range(E):
            dsend[g, i * slots:(i + 1) * slots] = d[:, g * tl:(g + 1) * tl]

    def expert_forward(i):
        v = nn(full_in[i], win[0])
        half, slope = gelu_parts(v)
        value = (v * half).astype(BF16)
        act[i] = value
        pre[i] = half + slope
        return value

    def expert_out(i, value):
        part_out[i] = nn(value, wout[0]).astype(BF16)
        return scatter(Z_OUT, i, part_out, rs_out)

    def every(ref):
        return ref[...].reshape(images * slots, ref.shape[-1])

    def expert_backward():
        grad_pre = (nt(every(full_grad), wout[0]) * every(pre)).astype(BF16)
        gpre[...] = grad_pre.reshape(gpre.shape)
        part_gin[...] = nt(grad_pre, win[0]).astype(BF16).reshape(part_gin.shape)

    colbuf[...] = jnp.zeros_like(colbuf)
    for i in range(images):
        statbuf[i, 8 * S:] = jnp.zeros_like(statbuf[i, 8 * S:])
    every_image = range(images)
    st, in_rs, grad_rs, in_ag, grad_ag = {}, {}, {}, {}, {}
    out_rs, gin_rs, out_ag, gin_ag = {}, {}, {}, {}
    emb_l.wait()
    emb_all[0] = emb[...]
    softmax(0)
    pl.semaphore_wait(barrier, S - 1 + E - 1)
    st[0], in_rs[0] = softmax_send(0)
    emb_ag = start([ecopy(E_EMB, k, emb_all.at[0], emb_all.at[k]) for k in range(1, E)])
    comb_l.wait()
    grad_rs[0] = out_grads(0)
    for i in range(1, images):
        softmax(i)
        st[i], in_rs[i] = softmax_send(i)
        in_ag[i - 1] = slot_inputs(i - 1, st[i - 1], in_rs[i - 1])
        grad_rs[i] = out_grads(i)
        dispatch(i - 1)
    last = images - 1
    in_ag[last] = slot_inputs(last, st[last], in_rs[last])
    dispatch(last)
    disp_all[0] = dsend[e]
    disp_a2a = start([ecopy(E_DISP, k, dsend.at[epeer[k]], disp_all.at[k]) for k in range(1, E)])
    for i in every_image:
        grad_ag[i] = sum_and_gather(grad_rs[i], Z_GRADF, i, part_grad, rs_grad, full_grad)

    win_l.wait()
    wout_l.wait()
    for i in every_image:
        arrive(in_ag[i])
        out_rs[i] = expert_out(i, expert_forward(i))
    stores.append(move(full_in, sin_h))
    stores.append(move(act, act_h))
    for i in every_image:
        arrive(grad_ag[i])
    expert_backward()
    for i in every_image:
        gin_rs[i] = scatter(Z_GIN, i, part_gin, rs_gin)
    for i in every_image:
        out_ag[i] = sum_and_gather(out_rs[i], Z_OUTF, i, part_out, rs_out, full_out)
    stores.append(move(full_grad, gso_h))
    stores.append(move(gpre, gpre_h))
    for i in every_image:
        gin_ag[i] = sum_and_gather(gin_rs[i], Z_GINF, i, part_gin, rs_gin, full_gin)

    per_row = 8 // images
    row_width = patches // per_row
    for i in every_image:
        arrive(out_ag[i])
        gc = nt(full_out[i], go[i])
        gcomb[i] = gc
        rd = jnp.sum(combt[i].astype(F32) * gc, axis=0, keepdims=True)
        for q in range(per_row):
            row_buf[0, i * per_row + q:i * per_row + q + 1] = rd[:, q * row_width:(q + 1) * row_width]
    row_x = start([ecopy(E_ROW, k, row_buf.at[0], row_buf.at[k]) for k in range(1, E)])

    direct = [1] + list(range(2, E, 2))
    gin_x, col_x = {}, {}
    for i in every_image:
        arrive(gin_ag[i])
        gin_all[i, 0] = full_gin[i]
        gin_x[i] = start([ecopy(E_GIN + i, k, gin_all.at[i, 0], gin_all.at[i, k]) for k in direct])
        gd = nt(full_gin[i], tok[i])
        gdisp[i] = gd
        cd = jnp.sum(disp[i].astype(F32) * gd, axis=1, keepdims=True)
        colbuf[0:slots] = jnp.broadcast_to(cd, (slots, 128))
        esend[i] = colbuf[...].T[0:8]
        col_x[i] = start([zcopy(Z_COL, i, k, esend.at[i], erecv.at[i, k - 1])
                          for k in range(1, S)])
    arrive(row_x)
    row_total = row_buf[0]
    for k in range(1, E):
        row_total = row_total + row_buf[k]
    for i in every_image:
        rd = jnp.concatenate(
            [row_total[i * per_row + q:i * per_row + q + 1] for q in range(per_row)], axis=1)
        gcomb[i] = combt[i].astype(F32) * (gcomb[i] - rd)
    grads = []
    for i in every_image:
        arrive(col_x[i])
        col_total = esend[i]
        for k in range(1, S):
            col_total = col_total + erecv[i, k - 1]
        colbuf[0:8] = col_total
        col_dot = colbuf[...].T[0:slots, 0:1]
        gl = (disp[i].astype(F32) * (gdisp[i] - col_dot) + gcomb[i]).astype(BF16)
        grads.append(gl)
        for g in range(E):
            lsend[g, i * slots:(i + 1) * slots] = gl[:, g * tl:(g + 1) * tl]
    log_all[0] = lsend[e]
    log_a2a = start([ecopy(E_LOG, k, lsend.at[epeer[k]], log_all.at[k]) for k in range(1, E)])

    forward = {}

    def hand_on(i):
        forward[i] = []
        for n, k in enumerate(direct):
            gin_x[i][n].wait_recv()
            if k > 1:
                forward[i] += start([
                    ecopy(E_GIN + i, k + 1, gin_all.at[i, k], gin_all.at[i, k + 1], to=1)])

    hand_on(0)
    embed_part = nn(grads[0], tok[0])
    for i in range(1, images):
        embed_part = embed_part + nn(grads[i], tok[i])
    embed_part = embed_part.astype(BF16)
    eo = width // S
    for g in range(S):
        embed_send[g] = embed_part[:, g * eo:(g + 1) * eo]
    embed_rs = start([zcopy(Z_EMB, 0, k, embed_send.at[zpeer[k]], embed_recv.at[k - 1])
                      for k in range(1, S)])

    for i in range(1, images):
        hand_on(i)
    arrive(disp_a2a)
    arrive(emb_ag)
    arrive(log_a2a)
    every_emb = emb_all[...].reshape(E * slots, width)
    span = [slice(i * slots, (i + 1) * slots) for i in every_image]
    logit_term = [tn(log_all[:, here].reshape(E * slots, tl), every_emb) for here in span]
    for i, here in enumerate(span):
        arrive(forward[i])
        total = logit_term[i] + tn(disp_all[:, here].reshape(E * slots, tl),
                           gin_all[i].reshape(E * slots, width))
        gt[i] = total.astype(BF16)
        stores.append(move(gt.at[i], gt_h.at[i]))
    arrive(embed_rs)
    total = embed_send[s].astype(F32)
    for k in range(1, S):
        total = total + embed_recv[k - 1].astype(F32)
    ge[...] = total.astype(BF16)
    stores.append(move(ge, ge_h))
    for c in sent:
        c.wait_send()
    for c in stores:
        c.wait()


def weights_kernel(steps, sin_h, gpre_h, act_h, gso_h, gt_h, ge_h,
                   gw_in_h, gw_out_h, gt_o, ge_o,
                   sin, gpre, act, gso, gt, ge, block_in, block_out, sems):
    images, slots, width = sin.shape
    rows = images * slots
    loads = [pltpu.make_async_copy(src, dst, sems.at[n]) for n, (src, dst) in enumerate(
        [(sin_h, sin), (gpre_h, gpre), (act_h, act), (gso_h, gso), (gt_h, gt), (ge_h, ge)])]
    for c in loads:
        c.start()
    n = len(loads)
    out = []
    for left_ref, right_ref, block, dst, first in (
            (sin, gpre, block_in, gw_in_h, 0), (act, gso, block_out, gw_out_h, 2)):
        loads[first].wait()
        loads[first + 1].wait()
        left = left_ref[...].reshape(rows, -1)
        right = right_ref[...].reshape(rows, -1)
        size = left.shape[1] // steps
        for b in range(steps):
            block[b] = tn(left[:, b * size:(b + 1) * size], right).astype(BF16)
            c = pltpu.make_async_copy(block.at[b], dst.at[0, pl.ds(b * size, size)], sems.at[n])
            n += 1
            c.start()
            out.append(c)
        if first == 0:
            for load, src, dst in ((loads[4], gt, gt_o), (loads[5], ge, ge_o)):
                load.wait()
                c = pltpu.make_async_copy(src, dst, sems.at[n])
                n += 1
                c.start()
                out.append(c)
    for c in out:
        c.wait()


def local(S, E, tokens, slot_embed, combine, w_in, w_out, grad_out):
    images, patches, width = tokens.shape
    slots = slot_embed.shape[1]
    hidden = w_in.shape[2]
    rows = images * slots
    own = rows // S
    tl = patches // E
    any_spec = pl.BlockSpec(memory_space=pl.ANY)
    vmem_spec = pl.BlockSpec(memory_space=pltpu.VMEM)

    def shape(*dims, dtype=BF16):
        return jax.ShapeDtypeStruct(dims, dtype)

    def vmem(*dims, dtype=BF16):
        return pltpu.VMEM(dims, dtype)

    flops = 2 * images * patches * slots * width * 7 + 8 * rows * width * hidden
    chunk = (images, S - 1, 16, slots * width // (16 * S))
    whole = (images, slots, width)
    inner = (images, slots, hidden)
    outs = (
        shape(images, tl, width), shape(slots, width // S), shape(*inner),
        shape(*whole), shape(*whole), shape(*inner),
    )
    gt, ge, act, gso, slot_in, gpre = pl.pallas_call(
        functools.partial(main_kernel, S, E),
        out_shape=outs,
        in_specs=[any_spec] * 6,
        out_specs=(any_spec,) * 6,
        scratch_shapes=[
            vmem(slots, width), vmem(*tokens.shape),
            vmem(*grad_out.shape), vmem(*w_in.shape), vmem(*w_out.shape),
            vmem(E, slots, width), vmem(E, rows, tl), vmem(images, E, slots, width),
            vmem(E, rows, tl), vmem(E, rows, tl), vmem(E, rows, tl),
            vmem(E, 8, images * patches // 8, dtype=F32),
            vmem(images, slots, patches, dtype=F32), vmem(images, slots, patches),
            vmem(images, slots, patches), vmem(images, slots, patches, dtype=F32),
            vmem(images, slots, patches, dtype=F32),
            vmem(images, S, slots, 128, dtype=F32), vmem(images, 128, 128, dtype=F32),
            vmem(128, 128, dtype=F32),
            vmem(*whole), vmem(*whole), vmem(*whole), vmem(*whole),
            vmem(*chunk), vmem(*chunk), vmem(*chunk), vmem(*chunk),
            vmem(*whole), vmem(*whole), vmem(*whole), vmem(*whole),
            vmem(*inner), vmem(*inner), vmem(images, tl, width), vmem(slots, width // S),
            vmem(*inner, dtype=F32),
            vmem(images, 8, 128, dtype=F32), vmem(images, S - 1, 8, 128, dtype=F32),
            vmem(S, slots, width // S), vmem(S - 1, slots, width // S),
            pltpu.SemaphoreType.DMA((Z_KINDS * images, S)),
            pltpu.SemaphoreType.DMA((Z_KINDS * images, S)),
            pltpu.SemaphoreType.DMA((E_GIN + images, E)),
            pltpu.SemaphoreType.DMA((E_GIN + images, E)),
            pltpu.SemaphoreType.DMA((9 + 3 * images,)),
        ],
        compiler_params=pltpu.CompilerParams(
            collective_id=0, has_side_effects=True, vmem_limit_bytes=56 * 2**20),
        cost_estimate=pl.CostEstimate(
            flops=flops, bytes_accessed=18 * 2**20, transcendentals=images * patches * slots),
        name="moe_backward",
    )(slot_embed.T, tokens, jnp.swapaxes(combine, 1, 2), grad_out, w_in, w_out)

    steps = 5 if width % (5 * 128) == 0 and hidden % (5 * 128) == 0 else 1
    gw_in, gw_out, gt, ge = pl.pallas_call(
        functools.partial(weights_kernel, steps),
        out_shape=(shape(1, width, hidden), shape(1, hidden, width)) + outs[:2],
        in_specs=[any_spec] * 6,
        out_specs=(any_spec,) * 4,
        scratch_shapes=[
            vmem(*whole), vmem(*inner), vmem(*inner), vmem(*whole),
            vmem(*outs[0].shape), vmem(*outs[1].shape),
            vmem(steps, width // steps, hidden), vmem(steps, hidden // steps, width),
            pltpu.SemaphoreType.DMA((8 + 2 * steps,)),
        ],
        compiler_params=pltpu.CompilerParams(vmem_limit_bytes=56 * 2**20),
        name="weight_gradients",
    )(slot_in, gpre, act, gso, gt, ge)
    return gt, ge.T, gw_in, gw_out


def solution(mesh):
    return jax.shard_map(
        functools.partial(local, mesh.shape["seq"], mesh.shape["expert"]),
        mesh=mesh,
        in_specs=(
            P(None, "seq", None),
            P(None, "expert"),
            P(None, "seq", "expert"),
            P("expert", None, "seq"),
            P("expert", "seq", None),
            P(None, "seq", None),
        ),
        out_specs=(
            P(None, ("seq", "expert"), None),
            P("seq", "expert"),
            P("expert", None, "seq"),
            P("expert", "seq", None),
        ),
        check_vma=False,
    )
```
